32 devices in a mesh: groups: 2 (over y), ep: 16 (over z, x, core).
Axes of the slice: x: 2, y: 2, z: 4, core: 2. Of those that a mesh axis runs over, the one named last changes fastest.
Arguments:
- hidden: bfloat16 [64, 7168], P(('groups', 'ep')), parts along dimension 0, may hold values from -6 to 6
- queries: bfloat16 [64, 128, 576], P(('groups', 'ep')), parts along dimension 0, may hold values from -40 to 40
- latent_cache: bfloat16 [64, 2048, 576], P(('groups', 'ep')), parts along dimension 0, may hold values from -8 to 8
- cache_lengths: int32 [64], P(('groups', 'ep')), parts along dimension 0, may hold values from 2 to 2048, as said below
- value_up: bfloat16 [128, 512, 128], P('ep'), may hold values from -0.25 to 0.25
- out_proj: bfloat16 [16384, 7168], P('ep'), may hold values from -0.046875 to 0.046875
- norm_gain: float32 [7168], replicated, may hold values from 0.1 to 1.9
- expert_ids: int32 [64, 8], P(('groups', 'ep')), parts along dimension 0, may hold values from 0 to 15, all different within a row; in each aligned block of 2 rows (0 to 1, 2 to 3, ...) at most 2 rows name the same one
- gate_weights: float32 [64, 8], P(('groups', 'ep')), parts along dimension 0, may hold values from 0.05 to 0.5
- gate_proj: bfloat16 [16, 7168, 1024], P('ep'), may hold values from -0.0625 to 0.0625
- up_proj: bfloat16 [16, 7168, 1024], P('ep'), may hold values from -0.0625 to 0.0625
- down_proj: bfloat16 [16, 1024, 7168], P('ep'), may hold values from -0.1875 to 0.1875
Outputs:
- layer_out: bfloat16 [64, 7168], P(('groups', 'ep')), parts along dimension 0
The draws below stay inside these ranges and needn't reach their ends.
There are 2 independent parts, one for each index of `groups`. The reference program is written for one: setup_inputs(seed, part) draws one part's arguments, and reference() takes and returns one part's arrays. A program takes and returns all parts, laid end to end along the dimension named above; an argument that names none is the same for every part. Nothing has to cross between parts.
Inputs may be any that keep to these rules, and one draw needn't show every extreme that they name: `cache_lengths`: some row of each draw has exactly 2048 live positions and some row exactly 2. `expert_ids`: each row names 8 different experts. The 2 rows of one device name any one expert at most 2 times, so a device sends each expert at most 2 rows; some device of every draw reaches that.
All inputs are finite; a program needn't handle non-finite values.
Results may differ from the reference program's by a relative error of at most 0.0095.
Values may be sent and summed in bfloat16 or wider, within the bound.
No kernel may reach another device: no remote copies, remote signals or barrier semaphores. Data moves between devices by JAX's collectives and lax.ppermute only.
A program may use at most 128 MiB of HBM per device.

```python
import math
import jax
import jax.numpy as jnp
import numpy as np
from jax import lax

D = 7168
FF = 1024
HEADS = 128
LAT = 512
VDIM = 128
EXPERTS = 16
TOPK = 8
ROWS_DEV = 2
CTX = 2048
KDIM = 576
ROWS = 32
SPLIT = 1
DSL = 7168


def cache_front(key):
    lead_keys = jax.random.normal(jax.random.fold_in(key, 11), (ROWS, 1, KDIM), jnp.float32)
    offset_noise = 0.3 * jax.random.normal(jax.random.fold_in(key, 12), (ROWS, 1, KDIM), jnp.float32)
    return (lead_keys, lead_keys + offset_noise)


def draw_latent_cache(key, part):
    lead_keys, near_keys = cache_front(key)
    remaining = jax.random.normal(jax.random.fold_in(key, 13), (ROWS, CTX - 2, KDIM), jnp.float32)
    return jnp.concatenate([lead_keys, near_keys, remaining], axis=1).astype(jnp.bfloat16)


def draw_queries(key, part):
    drawn_query = jax.random.normal(jax.random.fold_in(key, 21), (ROWS, HEADS, KDIM), jnp.float32)
    return drawn_query.astype(jnp.bfloat16)


def draw_cache_lengths(key, part):
    lengths = jax.random.randint(jax.random.fold_in(key, 31), (ROWS,), 2, CTX + 1, jnp.int32)
    long_row = jax.random.randint(jax.random.fold_in(key, 32), (), 0, ROWS, jnp.int32)
    step_over = jax.random.randint(jax.random.fold_in(key, 33), (), 0, ROWS - 1, jnp.int32)
    short_row = (long_row + 1 + step_over) % ROWS
    return lengths.at[long_row].set(CTX).at[short_row].set(2)


def block_levels(stream_key, extent, split, smallest, high):
    def one(axis_at, blocks):
        heights = jax.random.uniform(jax.random.fold_in(jax.random.fold_in(stream_key, 6), axis_at), (blocks,), jnp.float32, smallest / len(split), high / len(split))
        return jnp.repeat(jnp.exp(heights), extent[axis_at] // blocks).reshape((-1,) + (1,) * (len(extent) - axis_at - 1))

    level = one(*split[0])
    for cut in split[1:]:
        level = level * one(*cut)
    return level


def deal_out(rng, own, number, rows, count, top, limit, lean):
    sequence = jax.random.permutation(rng, count)
    crowded, common = shares(count, rows * top, limit, lean, True), shares(count, rows * top, limit, lean, False)
    places = jnp.arange(count)

    def named(sizes, turn):
        used = int((sizes > 0).sum())
        fixed = max(1, used // 4)
        shifted = fixed + (places - fixed + turn * (used - fixed)) % max(1, count - fixed)
        return jnp.zeros((count,), jnp.int32).at[sequence[jnp.where(places < fixed, places, shifted)]].set(jnp.asarray(sizes, jnp.int32))

    sizes = jnp.where(number % 4 == 0, named(crowded, number // 4), named(common, number - number // 4 - 1))
    mixed = jax.random.permutation(jax.random.fold_in(own, 3), count)
    giver, taker = mixed[0:count // 2 * 2:2], mixed[1:count // 2 * 2:2]
    slack = jnp.minimum(sizes[giver] - 1, limit - sizes[taker]) // 2
    slack = jnp.where((giver == sequence[0]) | (taker == sequence[0]) | (sizes[taker] == 0), 0, jnp.maximum(slack, 0))
    shifted = jax.random.randint(jax.random.fold_in(own, 4), (count // 2,), 0, 1 << 20) % (slack + 1)
    sizes = sizes.at[giver].add(-shifted).at[taker].add(shifted)
    items = jnp.searchsorted(jnp.cumsum(sizes), jnp.arange(rows * top), side="right").astype(jnp.int32)
    listing = items.reshape(top, rows).T
    listing = listing[jax.random.permutation(jax.random.fold_in(own, 1), rows)]
    turn = jax.random.randint(jax.random.fold_in(own, 2), (rows, 1), 0, top)
    return jnp.take_along_axis(listing, (jnp.arange(top)[None, :] + turn) % top, axis=1)


def shares(count, total, bound, slope, full):
    portions = [(1 << 20) // math.isqrt(standing ** slope) + 1 for standing in range(1, count + 1)]
    largest = bound if full else min(bound, max(-(-total // count), total * portions[0] // sum(portions)))
    least = 1 if total - largest >= count - 1 else 0
    counts, spare = [largest] + [least] * (count - 1), total - largest - least * (count - 1)
    while spare > 0:
        movable = [i for i in range(1, count) if counts[i] < largest] or [i for i in range(1, count) if counts[i] < bound]
        mass, left = sum([portions[i] for i in movable]), spare
        for i in movable:
            addition = min(bound - counts[i], max(1, left * portions[i] // mass), spare)
            counts[i] = counts[i] + addition
            spare = spare - addition
    return np.array(counts)


def bell_draw(own_key, dims, width, reach, pieces=(), kind=jnp.bfloat16):
    values = width * jax.random.normal(own_key, dims, jnp.float32)
    if pieces:
        values = values * block_levels(own_key, dims, pieces, -0.22, 0.18)
    return jnp.clip(values, -reach, reach).astype(kind)


def setup_inputs(seed: int = 0, part: int = 0) -> dict:
    seeds = jax.random.split(jax.random.key(seed), 13)
    part_keys = jax.random.split(jax.random.fold_in(seeds[12], part), 13)
    hidden = bell_draw(part_keys[0], (ROWS, D), 1.0, 6.0, ((0, 16),))
    queries = draw_queries(jax.random.fold_in(jax.random.fold_in(seeds[12], part), 71), part)
    latent_cache = draw_latent_cache(jax.random.fold_in(jax.random.fold_in(seeds[12], part), 71), part)
    cache_lengths = draw_cache_lengths(jax.random.fold_in(jax.random.fold_in(seeds[12], part), 71), part)
    value_up = bell_draw(seeds[4], (HEADS, LAT, VDIM), LAT ** -0.5, 0.25, ((0, 16),))
    out_proj = bell_draw(seeds[5], (HEADS * VDIM, D), (HEADS * VDIM) ** -0.5, 0.046875, ((0, 16),))
    norm_gain = jnp.clip(1.0 + 0.18 * jax.random.normal(seeds[6], (D,), jnp.float32), 0.1, 1.9)
    expert_ids_keys = jax.random.split(jax.random.fold_in(part_keys[7], 1), ROWS // ROWS_DEV)
    expert_ids_turns = jax.random.permutation(jax.random.fold_in(part_keys[7], 3), ROWS // ROWS_DEV)
    expert_ids = jax.vmap(lambda own, number: deal_out(jax.random.fold_in(part_keys[7], 2), own, number, ROWS_DEV, EXPERTS, TOPK, ROWS_DEV, 2))(expert_ids_keys, expert_ids_turns).reshape((ROWS, TOPK))
    gate_weights = jnp.clip(0.05 + 0.45 * jax.random.uniform(part_keys[8], (ROWS, TOPK), jnp.float32) ** block_levels(part_keys[8], (ROWS, TOPK), ((0, 16),), -0.2, 0.2), 0.05, 0.5)
    gate_proj = bell_draw(seeds[9], (SPLIT * EXPERTS, DSL, FF), D ** -0.5, 0.0625, ((0, 16),))
    up_proj = bell_draw(seeds[10], (SPLIT * EXPERTS, DSL, FF), D ** -0.5, 0.0625, ((0, 16),))
    down_proj = bell_draw(seeds[11], (SPLIT * EXPERTS, FF, DSL), FF ** -0.5, 0.1875, ((0, 16),))
    return dict(hidden=hidden, queries=queries, latent_cache=latent_cache, cache_lengths=cache_lengths, value_up=value_up, out_proj=out_proj, norm_gain=norm_gain, expert_ids=expert_ids, gate_weights=gate_weights, gate_proj=gate_proj, up_proj=up_proj, down_proj=down_proj)


score_scale = 0.07216878364870323
norm_eps = 1e-06

def attend(row_args):
    row_query, row_cache, row_length = row_args
    scores = jnp.dot(row_query, row_cache.T, preferred_element_type=jnp.float32) * score_scale
    live_mask = jnp.arange(CTX, dtype=jnp.int32) < row_length
    scores = jnp.where(live_mask[None, :], scores, -jnp.inf)
    row_peak = lax.optimization_barrier(jnp.max(scores, axis=1, keepdims=True))
    exp_scores = jnp.exp(scores - row_peak)
    soft_weights = (exp_scores / lax.optimization_barrier(jnp.sum(exp_scores, axis=1, keepdims=True))).astype(jnp.bfloat16)
    return jnp.dot(soft_weights, row_cache[:, :LAT], preferred_element_type=jnp.float32).astype(jnp.bfloat16)

def reference(hidden, queries, latent_cache, cache_lengths, value_up, out_proj, norm_gain, expert_ids, gate_weights, gate_proj, up_proj, down_proj):
    latent_out = lax.map(attend, (queries, latent_cache, cache_lengths))
    head_out = jnp.einsum('rhl,hlv->rhv', latent_out.astype(jnp.float32), value_up.astype(jnp.float32)).astype(jnp.bfloat16)
    attention = jnp.dot(head_out.reshape(ROWS, HEADS * VDIM), out_proj, preferred_element_type=jnp.float32)
    residual = hidden.astype(jnp.float32) + attention
    inv_rms = lax.rsqrt(lax.optimization_barrier(jnp.mean(residual * residual, axis=1, keepdims=True)) + norm_eps)
    moe_in = (residual * inv_rms * norm_gain[None, :]).astype(jnp.bfloat16)
    gate_full = gate_proj.reshape(SPLIT, EXPERTS, DSL, FF).transpose(1, 0, 2, 3).reshape(EXPERTS, D, FF)
    up_full = up_proj.reshape(SPLIT, EXPERTS, DSL, FF).transpose(1, 0, 2, 3).reshape(EXPERTS, D, FF)
    down_full = down_proj.reshape(SPLIT, EXPERTS, FF, DSL).transpose(1, 2, 0, 3).reshape(EXPERTS, FF, D)

    def expert_mlp(mats):
        gate_mat, up_mat, down_mat = mats
        gate_act = jnp.dot(moe_in, gate_mat, preferred_element_type=jnp.float32)
        up_act = jnp.dot(moe_in, up_mat, preferred_element_type=jnp.float32)
        units = (jax.nn.silu(gate_act) * up_act).astype(jnp.bfloat16)
        return jnp.dot(units, down_mat, preferred_element_type=jnp.float32).astype(jnp.bfloat16)
    stacked = lax.map(expert_mlp, (gate_full, up_full, down_full))
    one_hot = (expert_ids[:, :, None] == jnp.arange(EXPERTS, dtype=jnp.int32)[None, None, :]).astype(jnp.float32)
    weights_full = lax.optimization_barrier(jnp.sum(gate_weights[:, :, None] * one_hot, axis=1))
    routed_sum = jnp.einsum('re,erd->rd', weights_full, stacked.astype(jnp.float32))
    return (residual + routed_sum).astype(jnp.bfloat16)
```

```python
import jax
import jax.numpy as jnp
from jax import lax
from jax.sharding import PartitionSpec as P

EXPERTS = 16


score_scale = 0.07216878364870323
norm_eps = 1e-06


def partner(value, axis, bit):
    return lax.ppermute(value, axis, [(i, i ^ 1 << bit) for i in range(lax.axis_size(axis))])


def attend_and_project(hidden, queries, latent_cache, cache_lengths, value_up, out_proj):
    latent = value_up.shape[1]
    scores = (
        jnp.einsum("rhk,rtk->rht", queries, latent_cache, preferred_element_type=jnp.float32)
        * score_scale
    )
    positions = lax.broadcasted_iota(jnp.int32, scores.shape, 2)
    scores = jnp.where(positions < cache_lengths[:, None, None], scores, -jnp.inf)
    row_peak = jnp.max(scores, axis=2, keepdims=True)
    exp_scores = jnp.exp(scores - row_peak)
    soft_weights = (exp_scores / jnp.sum(exp_scores, axis=2, keepdims=True)).astype(jnp.bfloat16)
    latent_out = jnp.einsum(
        "rht,rtl->rhl",
        soft_weights,
        latent_cache[:, :, :latent],
        preferred_element_type=jnp.float32,
    ).astype(jnp.bfloat16)
    by_head = lax.all_to_all(latent_out, "ep", split_axis=1, concat_axis=0, tiled=True)
    head_out = jnp.einsum(
        "rhl,hlv->rhv", by_head, value_up, preferred_element_type=jnp.float32
    ).astype(jnp.bfloat16)
    head_rows = head_out.reshape(head_out.shape[0], head_out.shape[1] * head_out.shape[2])
    attention = lax.psum_scatter(
        jnp.dot(head_rows, out_proj, preferred_element_type=jnp.float32),
        "ep",
        scatter_dimension=0,
        tiled=True,
    )
    return hidden.astype(jnp.float32) + attention


def on_device(
    hidden,
    queries,
    latent_cache,
    cache_lengths,
    value_up,
    out_proj,
    norm_gain,
    expert_ids,
    gate_weights,
    gate_proj,
    up_proj,
    down_proj,
):
    rows_dev = hidden.shape[0]
    ep_size = lax.axis_size("ep")
    residual = attend_and_project(hidden, queries, latent_cache, cache_lengths, value_up, out_proj)
    inv_rms = lax.rsqrt(jnp.mean(residual * residual, axis=1, keepdims=True) + norm_eps)
    moe_in = (residual * inv_rms * norm_gain[None, :]).astype(jnp.bfloat16)
    split_ways = ep_size // EXPERTS
    slice_width = moe_in.shape[1] // split_ways
    experts_iota = lax.broadcasted_iota(jnp.int32, (1, 1, EXPERTS), 2)
    member = jnp.sum((expert_ids[:, :, None] == experts_iota).astype(jnp.int32), axis=1)
    row_iota = jnp.arange(rows_dev)
    earlier = (row_iota[None, :] < row_iota[:, None]).astype(jnp.int32)
    before = jnp.sum(earlier[:, :, None] * member[None, :, :], axis=1)
    slot_of = jnp.take_along_axis(before, expert_ids, axis=1)
    slot_iota = lax.broadcasted_iota(jnp.int32, (1, rows_dev, 1), 1)
    chosen = (member.T[:, None, :] == 1) & (before.T[:, None, :] == slot_iota)
    selection = chosen.astype(jnp.bfloat16)
    pieces = moe_in.reshape(rows_dev, split_ways, slice_width)
    outgoing = jnp.einsum(
        "ecr,rjd->jecd", selection, pieces, preferred_element_type=jnp.float32
    ).astype(jnp.bfloat16)
    outgoing = outgoing.reshape(ep_size, rows_dev, slice_width)
    incoming = lax.all_to_all(outgoing, "ep", split_axis=0, concat_axis=0, tiled=True)
    slot_rows = incoming.reshape(ep_size * rows_dev, slice_width)
    gate_act = jnp.dot(slot_rows, gate_proj[0], preferred_element_type=jnp.float32)
    up_act = jnp.dot(slot_rows, up_proj[0], preferred_element_type=jnp.float32)
    stacked = jnp.stack((gate_act, up_act))
    low_bit = EXPERTS.bit_length() - 1
    levels = split_ways.bit_length() - 1
    for swap_level in range(levels):
        stacked = stacked + partner(
            stacked.astype(jnp.bfloat16), "ep", low_bit + swap_level
        ).astype(stacked.dtype)
    hidden_units = (jax.nn.silu(stacked[0]) * stacked[1]).astype(jnp.bfloat16)
    expert_out = jnp.dot(hidden_units, down_proj[0], preferred_element_type=jnp.float32).astype(
        jnp.bfloat16
    )
    expert_out = expert_out.reshape(ep_size, rows_dev, slice_width)
    returned = lax.all_to_all(expert_out, "ep", split_axis=0, concat_axis=0, tiled=True)
    full_rows = returned.reshape(split_ways, EXPERTS, rows_dev, slice_width).transpose(1, 2, 0, 3)
    full_rows = full_rows.reshape(EXPERTS * rows_dev, split_ways * slice_width)
    picked = jnp.take(full_rows, expert_ids * rows_dev + slot_of, axis=0)
    routed_sum = jnp.sum(gate_weights[:, :, None] * picked.astype(jnp.float32), axis=1)
    return (residual + routed_sum).astype(jnp.bfloat16)


def solution(mesh):
    return jax.shard_map(
        on_device,
        mesh=mesh,
        in_specs=(
            P(("groups", "ep"), None),
            P(("groups", "ep"), None, None),
            P(("groups", "ep"), None, None),
            P(("groups", "ep")),
            P("ep", None, None),
            P("ep", None),
            P(),
            P(("groups", "ep"), None),
            P(("groups", "ep"), None),
            P("ep", None, None),
            P("ep", None, None),
            P("ep", None, None),
        ),
        out_specs=P(("groups", "ep"), None),
        check_vma=False,
    )
```

```python
import jax
import jax.numpy as jnp
from jax import lax
from jax.sharding import PartitionSpec as P

EXPERTS = 16


score_scale = 0.07216878364870323
norm_eps = 1e-06


def exchange(value, bit):
    return lax.ppermute(value, "ep", [(i, i ^ (1 << bit)) for i in range(lax.axis_size("ep"))])


def halve(value, bit):
    kept, sent = jnp.split(value, 2, axis=0)
    return kept + exchange(sent.astype(jnp.bfloat16), bit).astype(jnp.float32)


def relative_order(bits):
    return [sum(((p >> (bits - 1 - b)) & 1) << b for b in range(bits)) for p in range(1 << bits)]


def attend(queries, latent_cache, cache_lengths, latent):
    scores = (
        jnp.einsum("rhk,rtk->rht", queries, latent_cache, preferred_element_type=jnp.float32)
        * score_scale
    )
    positions = lax.broadcasted_iota(jnp.int32, scores.shape, 2)
    scores = jnp.where(positions < cache_lengths[:, None, None], scores, -jnp.inf)
    row_peak = jnp.max(scores, axis=2, keepdims=True)
    exp_scores = jnp.exp(scores - row_peak)
    soft_weights = (exp_scores / jnp.sum(exp_scores, axis=2, keepdims=True)).astype(jnp.bfloat16)
    return jnp.einsum(
        "rht,rtl->rhl",
        soft_weights,
        latent_cache[:, :, :latent],
        preferred_element_type=jnp.float32,
    ).astype(jnp.bfloat16)


def on_device(
    hidden,
    queries,
    latent_cache,
    cache_lengths,
    value_up,
    out_proj,
    norm_gain,
    expert_ids,
    gate_weights,
    gate_proj,
    up_proj,
    down_proj,
):
    rows_dev, width = hidden.shape
    heads_dev, latent, _ = value_up.shape
    ep_size = lax.axis_size("ep")
    me = lax.axis_index("ep")
    bits = ep_size.bit_length() - 1
    split_ways = ep_size // EXPERTS
    scatter_bits = min(2, bits)

    latent_out = attend(queries, latent_cache, cache_lengths, latent)

    experts_iota = lax.broadcasted_iota(jnp.int32, (1, 1, EXPERTS), 2)
    named = expert_ids[:, :, None] == experts_iota
    weight = jnp.sum(jnp.where(named, gate_weights[:, :, None], 0.0), axis=1)
    weight = jnp.tile(weight, (1, split_ways))
    weight_top = weight.astype(jnp.bfloat16)
    weight_rest = (weight - weight_top.astype(jnp.float32)).astype(jnp.bfloat16)
    tail = jnp.stack((weight_top, weight_rest), axis=2)
    tail = jnp.pad(tail, ((0, 0), (0, 0), (0, 126)))
    outgoing = latent_out.reshape(rows_dev, ep_size, heads_dev * latent)
    outgoing = jnp.concatenate((outgoing, tail), axis=2).transpose(1, 0, 2)
    incoming = lax.all_to_all(outgoing, "ep", split_axis=0, concat_axis=0, tiled=True)

    order = jnp.array(relative_order(bits), jnp.int32)
    place = (jnp.arange(ep_size)[None, :] == (order ^ me)[:, None]).astype(jnp.float32)
    place = jnp.kron(place, jnp.eye(rows_dev, dtype=jnp.float32)).astype(jnp.bfloat16)
    incoming = incoming.reshape(ep_size * rows_dev, -1)
    rows_in = incoming.shape[0]
    by_head = incoming[:, : heads_dev * latent].reshape(rows_in, heads_dev, latent)
    head_out = jnp.einsum(
        "rhl,hlv->rhv", by_head, value_up, preferred_element_type=jnp.float32
    ).astype(jnp.bfloat16)
    head_rows = jnp.dot(
        place, head_out.reshape(rows_in, -1), preferred_element_type=jnp.float32
    ).astype(jnp.bfloat16)
    tail_in = jnp.dot(
        place, incoming[:, heads_dev * latent :], preferred_element_type=jnp.float32
    )
    row_weight = tail_in[:, 0:1] + tail_in[:, 1:2]

    summed = jnp.dot(head_rows, out_proj, preferred_element_type=jnp.float32)
    own = summed[:rows_dev] + hidden.astype(jnp.float32)
    summed = jnp.concatenate((own, summed[rows_dev:]), axis=0)
    for bit in range(scatter_bits):
        summed = halve(summed, bit)
    for bit in range(scatter_bits, bits):
        shape = summed.shape
        swapped = summed.astype(jnp.bfloat16).reshape(1 << (bit - scatter_bits), 2, -1, width)
        swapped = jnp.concatenate((swapped[:, 1:], swapped[:, :1]), axis=1).reshape(shape)
        summed = summed + exchange(swapped, bit).astype(jnp.float32)
    residual = summed[:rows_dev]
    inv_rms = lax.rsqrt(jnp.mean(summed * summed, axis=1, keepdims=True) + norm_eps)
    moe_in = (summed * inv_rms * norm_gain[None, :]).astype(jnp.bfloat16)
    for bit in reversed(range(scatter_bits)):
        moe_in = jnp.concatenate((moe_in, exchange(moe_in, bit)), axis=0)

    slice_width = width // split_ways
    part = me // EXPERTS
    if split_ways > 1:
        moe_in = lax.dynamic_slice_in_dim(moe_in, part * slice_width, slice_width, axis=1)
    gate_act = jnp.dot(moe_in, gate_proj[0], preferred_element_type=jnp.float32)
    up_act = jnp.dot(moe_in, up_proj[0], preferred_element_type=jnp.float32)
    if split_ways > 1:
        to_one = place.astype(jnp.float32)
        stacked = jnp.stack((gate_act, up_act)).astype(jnp.bfloat16).astype(jnp.float32)
        stacked = jnp.einsum("sr,asf->arf", to_one, stacked)
        for bit in range(EXPERTS.bit_length() - 1, bits):
            stacked = stacked + exchange(stacked.astype(jnp.bfloat16), bit).astype(jnp.float32)
        stacked = jnp.einsum("sr,arf->asf", to_one, stacked, precision=lax.Precision.HIGHEST)
        gate_act, up_act = stacked[0], stacked[1]
    units = (jax.nn.silu(gate_act) * up_act).astype(jnp.bfloat16)
    weighted = jnp.dot(units, down_proj[0], preferred_element_type=jnp.float32) * row_weight
    if split_ways > 1:
        wide = jnp.zeros((rows_in, width), jnp.float32)
        weighted = lax.dynamic_update_slice_in_dim(wide, weighted, part * slice_width, axis=1)
    for bit in range(bits):
        weighted = halve(weighted, bit)
    return (residual + weighted).astype(jnp.bfloat16)


def solution(mesh):
    return jax.shard_map(
        on_device,
        mesh=mesh,
        in_specs=(
            P(("groups", "ep"), None),
            P(("groups", "ep"), None, None),
            P(("groups", "ep"), None, None),
            P(("groups", "ep")),
            P("ep", None, None),
            P("ep", None),
            P(),
            P(("groups", "ep"), None),
            P(("groups", "ep"), None),
            P("ep", None, None),
            P("ep", None, None),
            P("ep", None, None),
        ),
        out_specs=P(("groups", "ep"), None),
        check_vma=False,
    )
```

```python
import functools

import jax
import jax.numpy as jnp
from jax import lax
from jax.experimental import pallas as pl
from jax.experimental.pallas import tpu as pltpu
from jax.sharding import PartitionSpec as P

EXPERTS = 16


score_scale = 0.07216878364870323
norm_eps = 1e-06


def exchange(value, bit):
    return trade(value, 1 << bit)


def trade(value, mask):
    return lax.ppermute(value, "ep", [(i, i ^ mask) for i in range(lax.axis_size("ep"))])


def relative_order(bits):
    return [sum(((p >> (bits - 1 - b)) & 1) << b for b in range(bits)) for p in range(1 << bits)]


LANES = 128
MIB = 1 << 20
IN_VMEM = pl.BlockSpec(memory_space=pltpu.VMEM)
IN_SMEM = pl.BlockSpec(memory_space=pltpu.SMEM)
IN_HBM = pl.BlockSpec(memory_space=pltpu.HBM)
VMEM_ARRAY = pltpu.VMEM


def in_vmem(value):
    return pltpu.with_memory_space_constraint(value, pltpu.VMEM)


def in_hbm(value):
    return pltpu.with_memory_space_constraint(value, pltpu.HBM)


def pieces(source, target, sems, first):
    count = sems.shape[0] - first
    run = source.shape[0] // count
    return [
        pltpu.make_async_copy(
            source.at[pl.ds(i * run, run)], target.at[pl.ds(i * run, run)], sems.at[first + i]
        )
        for i in range(count)
    ]


def load_kernel(source, after, target, sems):
    copies = pieces(source, target, sems, 0)
    for copy in copies:
        copy.start()
    for copy in copies:
        copy.wait()


def load(source, after):
    return pl.pallas_call(
        load_kernel,
        out_shape=VMEM_ARRAY(source.shape, source.dtype),
        in_specs=[IN_HBM, IN_VMEM],
        out_specs=IN_VMEM,
        scratch_shapes=[pltpu.SemaphoreType.DMA((4,))],
        compiler_params=pltpu.CompilerParams(vmem_limit_bytes=MIB),
        cost_estimate=pl.CostEstimate(
            flops=0, bytes_accessed=2 * source.size * source.dtype.itemsize, transcendentals=0
        ),
    )(in_hbm(source), in_vmem(after))


def attend_kernel(
    order, lengths, me, queries, cache, proj, value_up, kept, sent, proj_in, value_in, held, wide, sems
):
    rows_dev, _, heads = queries.shape
    context = cache.shape[2]
    latent = wide.shape[-1]
    caches = [pltpu.make_async_copy(cache.at[r], held.at[r], sems.at[r]) for r in range(rows_dev)]
    weights = [pltpu.make_async_copy(value_up, value_in, sems.at[rows_dev])]
    weights += pieces(proj, proj_in, sems, rows_dev + 1)
    for copy in caches + weights:
        copy.start()
    for r in range(rows_dev):
        caches[r].wait()
        scores = score_scale * lax.dot_general(
            queries[r], held[r], (((0,), (0,)), ((), ())), preferred_element_type=jnp.float32
        )
        positions = lax.broadcasted_iota(jnp.int32, (heads, context), 1)
        scores = jnp.where(positions < lengths[r], scores, -jnp.inf)
        exp_scores = jnp.exp(scores - jnp.max(scores, axis=1, keepdims=True))
        inverse = 1.0 / jnp.sum(exp_scores, axis=1, keepdims=True)
        soft_weights = (exp_scores * inverse).astype(jnp.bfloat16)
        got = lax.dot_general(
            soft_weights,
            held[r, :latent],
            (((1,), (1,)), ((), ())),
            preferred_element_type=jnp.float32,
        )
        if order:
            per = wide.shape[1] // rows_dev
            wide[:, r * per : (r + 1) * per] = got.reshape(-1, per, latent)
        else:
            kept[r] = got.astype(kept.dtype)
    half = len(order) // 2
    for p, s in enumerate(order):
        target = (kept, sent)[p // half]
        target[p % half] = wide[me[0] ^ s].astype(target.dtype)
    for copy in weights:
        copy.wait()


def attend(queries, latent_cache, cache_lengths, out_proj, value_up, order, me):
    rows_dev, heads, key_width = queries.shape
    context = latent_cache.shape[1]
    heads_dev, latent, _ = value_up.shape
    shape = (len(order) // 2, rows_dev * heads_dev, latent) if order else (rows_dev, heads, latent)
    wide = (max(2 * shape[0], 1), shape[1], latent) if order else (1, 8, latent)
    spare = shape if order else (1, 16, latent)
    return pl.pallas_call(
        functools.partial(attend_kernel, order),
        out_shape=(
            VMEM_ARRAY(shape, jnp.bfloat16),
            VMEM_ARRAY(spare, jnp.bfloat16),
            VMEM_ARRAY(out_proj.shape, out_proj.dtype),
            VMEM_ARRAY(value_up.shape, value_up.dtype),
        ),
        in_specs=[IN_SMEM, IN_SMEM, IN_VMEM, IN_HBM, IN_HBM, IN_HBM],
        out_specs=(IN_VMEM,) * 4,
        scratch_shapes=[
            pltpu.VMEM((rows_dev, key_width, context), jnp.bfloat16),
            pltpu.VMEM(wide, jnp.float32),
            pltpu.SemaphoreType.DMA((rows_dev + 5,)),
        ],
        compiler_params=pltpu.CompilerParams(vmem_limit_bytes=24 * MIB),
    )(
        cache_lengths,
        me[None],
        queries.transpose(0, 2, 1),
        in_hbm(latent_cache.transpose(0, 2, 1)),
        in_hbm(out_proj),
        in_hbm(value_up),
    )


def dealt(sources, ways, run):
    return [
        [
            (a, (g * ways + i) * run)
            for a, blocks in enumerate(sources)
            for g in range(blocks // (ways * run))
        ]
        for i in range(ways)
    ]


def deal_kernel(plan, run, count, *refs):
    sources, targets = refs[:count], refs[-len(plan) :]
    for target, runs in zip(targets, plan):
        for j, (a, first) in enumerate(runs):
            target[j * run : (j + 1) * run] = sources[a][first : first + run]


def deal(sources, ways, run):
    plan = dealt([a.shape[0] for a in sources], ways, run)
    shape = (len(plan[0]) * run, *sources[0].shape[1:])
    return pl.pallas_call(
        functools.partial(deal_kernel, plan, run, len(sources)),
        out_shape=tuple(jax.ShapeDtypeStruct(shape, sources[0].dtype) for _ in plan),
        in_specs=[IN_VMEM] * len(sources),
        out_specs=(IN_VMEM,) * ways,
        compiler_params=pltpu.CompilerParams(vmem_limit_bytes=4 * MIB),
    )(*sources)


def project_kernel(
    tile, count, *refs
):
    row_of, value_up, proj, hidden, tail = refs[count : count + 5]
    kept, sent = refs[-2:]
    heads_dev = value_up.shape[0]
    half, wide = kept.shape
    rows_dev, width = hidden.shape
    maps = jnp.concatenate([value_up[h] for h in range(heads_dev)], axis=1)
    by_head = jnp.concatenate([a[...].reshape(-1, a.shape[-1]) for a in refs[:count]], axis=0)
    mixed = jnp.dot(by_head, maps, preferred_element_type=jnp.float32)
    row_head = lax.rem(lax.broadcasted_iota(jnp.int32, mixed.shape, 0), heads_dev)
    value_dim = value_up.shape[2]
    column_head = lax.broadcasted_iota(jnp.int32, mixed.shape, 1) // value_dim
    mixed = jnp.where(row_head == column_head, mixed, 0.0).astype(jnp.bfloat16)
    source = lax.broadcasted_iota(jnp.int32, (2 * half, mixed.shape[0]), 1) // heads_dev
    select = (row_of[...] == source).astype(jnp.bfloat16)
    head_rows = jnp.dot(select, mixed, preferred_element_type=jnp.float32)
    head_rows = head_rows.astype(jnp.bfloat16)

    @pl.loop(0, width // tile)
    def _(i):
        columns = pl.ds(pl.multiple_of(i * tile, tile), tile)
        terms = jnp.dot(head_rows, proj[:, columns], preferred_element_type=jnp.float32)
        kept[:, columns] = terms[:half]
        kept[0:rows_dev, columns] += hidden[:, columns].astype(jnp.float32)
        sent[:, columns] = terms[half:].astype(sent.dtype)

    kept[:, width:] = jnp.zeros((half, wide - width), kept.dtype)
    kept[0:rows_dev, width:] = tail[...]
    sent[:, width:] = jnp.zeros((half, wide - width), sent.dtype)


def project(by_head, row_of, value_up, out_proj, hidden, tail):
    rows_in = row_of.shape[0]
    width = hidden.shape[1]
    shape = (rows_in // 2, width + LANES)
    return pl.pallas_call(
        functools.partial(project_kernel, 512, len(by_head)),
        out_shape=(
            jax.ShapeDtypeStruct(shape, jnp.float32),
            jax.ShapeDtypeStruct(shape, jnp.bfloat16),
        ),
        in_specs=[IN_VMEM] * (len(by_head) + 5),
        out_specs=(IN_VMEM, IN_VMEM),
        compiler_params=pltpu.CompilerParams(vmem_limit_bytes=8 * MIB),
    )(
        *by_head,
        row_of,
        in_vmem(value_up),
        in_vmem(out_proj),
        hidden,
        tail,
    )


def halve_kernel(kept, got, next_kept, sent):
    half = sent.shape[0]
    total = kept[...] + got[...].astype(jnp.float32)
    next_kept[...] = total[:half]
    sent[...] = total[half:].astype(sent.dtype)


def swap_kernel(shift, kept, got, total_ref, sent):
    total = kept[...] + got[...].astype(jnp.float32)
    rows = total.shape[0]
    row = lax.broadcasted_iota(jnp.int32, total.shape, 0)
    later, earlier = pltpu.roll(total, rows - shift, 0), pltpu.roll(total, shift, 0)
    total_ref[...] = total
    sent[...] = jnp.where((row & shift) == 0, later, earlier).astype(sent.dtype)


def combine(kernel, kept, got, out_rows):
    shape = (out_rows, kept.shape[1])
    return pl.pallas_call(
        kernel,
        out_shape=(
            jax.ShapeDtypeStruct(shape, jnp.float32),
            jax.ShapeDtypeStruct(shape, jnp.bfloat16),
        ),
        in_specs=[IN_VMEM] * 2,
        out_specs=(IN_VMEM, IN_VMEM),
        compiler_params=pltpu.CompilerParams(
            vmem_limit_bytes=2 * MIB + 24 * kept.size
        ),
    )(kept, got)


def norm_kernel(kept, got, gain, residual, moe_in):
    rows_dev, width = residual.shape
    total = kept[...] + got[...].astype(jnp.float32)
    body = total[:, :width]
    square = jnp.mean(body * body, axis=1, keepdims=True)
    residual[...] = body[:rows_dev]
    moe_in[:, :width] = (body * lax.rsqrt(square + norm_eps) * gain[...]).astype(moe_in.dtype)
    moe_in[:, width:] = total[:, width:].astype(moe_in.dtype)


def norm(kept, got, gain, rows_dev):
    return pl.pallas_call(
        norm_kernel,
        out_shape=(
            jax.ShapeDtypeStruct((rows_dev, gain.shape[1]), jnp.float32),
            jax.ShapeDtypeStruct(kept.shape, jnp.bfloat16),
        ),
        in_specs=[IN_VMEM] * 3,
        out_specs=(IN_VMEM, IN_VMEM),
        compiler_params=pltpu.CompilerParams(
            vmem_limit_bytes=2 * MIB + 24 * kept.size
        ),
    )(kept, got, gain)


def stack_kernel(first, second, out):
    rows = first.shape[0]
    out[:rows] = first[...]
    out[rows:] = second[...]


def stack(first, second):
    shape = (2 * first.shape[0], first.shape[1])
    return pl.pallas_call(
        stack_kernel,
        out_shape=jax.ShapeDtypeStruct(shape, first.dtype),
        in_specs=[IN_VMEM] * 2,
        out_specs=IN_VMEM,
        compiler_params=pltpu.CompilerParams(vmem_limit_bytes=2 * MIB + 8 * first.size),
    )(first, second)


def strips(source, target, sems):
    count = sems.shape[0]
    run = source.shape[1] // count
    return [
        pltpu.make_async_copy(
            source.at[:, pl.ds(i * run, run)], target.at[:, pl.ds(i * run, run)], sems.at[i]
        )
        for i in range(count)
    ]


def expert_kernel(
    expert, first, second, gate, up, down, kept, sent, moe_in, gates, units, up_in, down_in, up_sems, down_sems
):
    width, inner = gate.shape
    half = kept.shape[0]
    ups, downs = strips(up, up_in, up_sems), strips(down, down_in, down_sems)
    for copy in ups:
        copy.start()
    moe_in[:half] = first[...]
    moe_in[half:] = second[...]
    rows = moe_in[:, :width]
    strip = inner // len(ups)
    tail = moe_in[:, width:].astype(jnp.float32)
    column = lax.broadcasted_iota(jnp.int32, tail.shape, 1)
    mine = (column == expert[0]) | (column == expert[0] + EXPERTS)
    weight = jnp.sum(jnp.where(mine, tail, 0.0), axis=1, keepdims=True)

    @pl.loop(0, len(ups))
    def _(i):
        columns = pl.ds(pl.multiple_of(i * strip, strip), strip)
        gate_act = jnp.dot(rows, gate[:, columns], preferred_element_type=jnp.float32)
        gates[:, columns] = jax.nn.silu(gate_act)

    later = iter(downs)
    for i, copy in enumerate(ups):
        copy.wait()
        next(later).start()
        columns = slice(i * strip, (i + 1) * strip)
        up_act = jnp.dot(rows, up_in[:, columns], preferred_element_type=jnp.float32)
        units[:, columns] = (gates[:, columns] * up_act).astype(units.dtype)
    strip = width // len(downs)
    for i, copy in enumerate(downs):
        copy.wait()
        for ahead in later:
            ahead.start()
            break
        columns = slice(i * strip, (i + 1) * strip)
        terms = weight * jnp.dot(
            units[...], down_in[:, columns], preferred_element_type=jnp.float32
        )
        kept[:, columns] = terms[:half]
        sent[:, columns] = terms[half:].astype(sent.dtype)


def run_expert(expert, first, second, gate, up, down):
    rows = 2 * first.shape[0]
    width, inner = gate.shape
    shape = (rows // 2, width)
    return pl.pallas_call(
        expert_kernel,
        out_shape=(
            jax.ShapeDtypeStruct(shape, jnp.float32),
            jax.ShapeDtypeStruct(shape, jnp.bfloat16),
        ),
        in_specs=[IN_SMEM] + [IN_VMEM] * 3 + [IN_HBM] * 2,
        out_specs=(IN_VMEM, IN_VMEM),
        scratch_shapes=[
            pltpu.VMEM((rows, first.shape[1]), jnp.bfloat16),
            pltpu.VMEM((rows, inner), jnp.float32),
            pltpu.VMEM((rows, inner), jnp.bfloat16),
            pltpu.VMEM(up.shape, up.dtype),
            pltpu.VMEM(down.shape, down.dtype),
            pltpu.SemaphoreType.DMA((4,)),
            pltpu.SemaphoreType.DMA((7,)),
        ],
        compiler_params=pltpu.CompilerParams(
            vmem_limit_bytes=4 * MIB + 4 * width * inner + 64 * rows * inner
        ),
    )(expert, first, second, in_vmem(gate), in_hbm(up), in_hbm(down))


def on_device(
    hidden,
    queries,
    latent_cache,
    cache_lengths,
    value_up,
    out_proj,
    norm_gain,
    expert_ids,
    gate_weights,
    gate_proj,
    up_proj,
    down_proj,
):
    rows_dev, width = hidden.shape
    ep_size = lax.axis_size("ep")
    me = lax.axis_index("ep")
    bits = ep_size.bit_length() - 1
    split_ways = ep_size // EXPERTS
    scatter_bits = min(2, bits)
    heads_dev, latent, _ = value_up.shape
    rows_in = ep_size * rows_dev

    experts_iota = lax.broadcasted_iota(jnp.int32, (1, 1, EXPERTS), 2)
    named = expert_ids[:, :, None] == experts_iota
    weight = jnp.sum(jnp.where(named, gate_weights[:, :, None], 0.0), axis=1)
    weight_top = weight.astype(jnp.bfloat16).astype(jnp.float32)
    weight_rest = (weight - weight_top).astype(jnp.bfloat16).astype(jnp.float32)
    tail = jnp.concatenate((weight_top, weight_rest), axis=1)
    tail = jnp.pad(tail, ((0, 0), (0, LANES - tail.shape[1])))

    order = relative_order(bits)
    gate, up, down = gate_proj[0], up_proj[0], down_proj[0]
    if heads_dev % 8 == 0:
        kept, sent, out_proj, value_up = attend(
            queries, latent_cache, cache_lengths, out_proj, value_up, order, me
        )
        run = ep_size >> 2
        got = exchange(sent, 0)
        kept, sent = deal((kept, got), 2, run)
        got = exchange(sent, 1)
        parts = deal((kept, got), run, 1)
        masks = order[:run]
        by_head = [parts[0]] + [trade(part, mask) for part, mask in zip(parts[1:], masks[1:])]
        held = [mask | x << 1 | core for mask in masks for x in range(2) for core in range(2)]
        row_of = jnp.array([held.index(s) * rows_dev + r for s in order for r in range(rows_dev)])
    else:
        out, _, out_proj, value_up = attend(
            queries, latent_cache, cache_lengths, out_proj, value_up, (), me
        )
        out = out.reshape(rows_dev, ep_size, heads_dev, latent).transpose(1, 0, 2, 3)
        by_head = [lax.all_to_all(out, "ep", split_axis=0, concat_axis=0, tiled=True)]
        by_head = [by_head[0].reshape(rows_in * heads_dev, latent)]
        row_of = (jnp.array(order) ^ me)[:, None] * rows_dev + jnp.arange(rows_dev)[None, :]
        row_of = row_of.reshape(-1)
    row_of = row_of.astype(jnp.int32)
    kept, sent = project(by_head, row_of[:, None], value_up, out_proj, hidden, tail)

    rows = rows_in // 2
    for bit in range(scatter_bits - 1):
        rows //= 2
        kept, sent = combine(halve_kernel, kept, exchange(sent, bit), rows)
    got = exchange(sent, scatter_bits - 1)
    for bit in range(scatter_bits, bits):
        shift = rows_dev << (bits - 1 - bit)
        kept, sent = combine(functools.partial(swap_kernel, shift), kept, got, rows)
        got = exchange(sent, bit)
    residual, moe_in = norm(kept, got, norm_gain[None, :], rows_dev)
    for bit in reversed(range(1, scatter_bits)):
        got = exchange(moe_in, bit)
        moe_in = stack(moe_in, got)
    if split_ways == 1:
        gate = load(gate, moe_in)
    other = exchange(moe_in, 0)

    expert = me % EXPERTS
    if split_ways == 1:
        kept, sent = run_expert(expert[None], moe_in, other, gate, up, down)
    else:
        moe_in = jnp.concatenate((moe_in, other), axis=0)
        tail_in = moe_in[:, width:].astype(jnp.float32)
        column = lax.broadcasted_iota(jnp.int32, tail_in.shape, 1)
        mine = (column == expert) | (column == expert + EXPERTS)
        row_weight = jnp.sum(jnp.where(mine, tail_in, 0.0), axis=1, keepdims=True)
        slice_width = width // split_ways
        start = (me // EXPERTS) * slice_width
        part_in = lax.dynamic_slice_in_dim(moe_in, start, slice_width, axis=1)
        gate_act = jnp.dot(part_in, gate, preferred_element_type=jnp.float32)
        up_act = jnp.dot(part_in, up, preferred_element_type=jnp.float32)
        to_one = (row_of[:, None] == jnp.arange(rows_in)[None, :]).astype(jnp.float32)
        stacked = jnp.stack((gate_act, up_act)).astype(jnp.bfloat16).astype(jnp.float32)
        stacked = jnp.einsum("sr,asf->arf", to_one, stacked)
        for bit in range(EXPERTS.bit_length() - 1, bits):
            stacked = stacked + exchange(stacked.astype(jnp.bfloat16), bit).astype(jnp.float32)
        stacked = jnp.einsum("sr,arf->asf", to_one, stacked, precision=lax.Precision.HIGHEST)
        units = (jax.nn.silu(stacked[0]) * stacked[1]).astype(jnp.bfloat16)
        weighted = jnp.dot(units, down, preferred_element_type=jnp.float32) * row_weight
        spread = jnp.zeros((rows_in, width), jnp.float32)
        spread = lax.dynamic_update_slice_in_dim(spread, weighted, start, axis=1)
        kept, sent = spread[: rows_in // 2], spread[rows_in // 2 :].astype(jnp.bfloat16)
    rows = rows_in // 2
    for bit in range(bits - 1):
        rows //= 2
        kept, sent = combine(halve_kernel, kept, exchange(sent, bit), rows)
    routed = kept + exchange(sent, bits - 1).astype(jnp.float32)
    return (residual + routed).astype(jnp.bfloat16)


def solution(mesh):
    return jax.shard_map(
        on_device,
        mesh=mesh,
        in_specs=(
            P(("groups", "ep"), None),
            P(("groups", "ep"), None, None),
            P(("groups", "ep"), None, None),
            P(("groups", "ep")),
            P("ep", None, None),
            P("ep", None),
            P(),
            P(("groups", "ep"), None),
            P(("groups", "ep"), None),
            P("ep", None, None),
            P("ep", None, None),
            P("ep", None, None),
        ),
        out_specs=P(("groups", "ep"), None),
        check_vma=False,
    )
```

```python
import functools

import jax
import jax.numpy as jnp
from jax import lax
from jax.experimental import pallas as pl
from jax.experimental.pallas import tpu as pltpu
from jax.sharding import PartitionSpec as P

EXPERTS = 16


score_scale = 0.07216878364870323
norm_eps = 1e-06


def exchange(value, bit):
    return trade(value, 1 << bit)


def trade(value, mask):
    return lax.ppermute(value, "ep", [(i, i ^ mask) for i in range(lax.axis_size("ep"))])


def relative_order(bits):
    return [sum(((p >> (bits - 1 - b)) & 1) << b for b in range(bits)) for p in range(1 << bits)]


LANES = 128
MIB = 1 << 20
IN_VMEM = pl.BlockSpec(memory_space=pltpu.VMEM)
IN_SMEM = pl.BlockSpec(memory_space=pltpu.SMEM)
ANYWHERE = pl.BlockSpec(memory_space=pl.ANY)
IN_HBM = pl.BlockSpec(memory_space=pltpu.HBM)
VMEM_ARRAY = pltpu.VMEM


def in_vmem(value):
    return pltpu.with_memory_space_constraint(value, pltpu.VMEM)


def in_hbm(value):
    return pltpu.with_memory_space_constraint(value, pltpu.HBM)


def pieces(source, target, sems, first):
    count = sems.shape[0] - first
    run = source.shape[0] // count
    return [
        pltpu.make_async_copy(
            source.at[pl.ds(i * run, run)], target.at[pl.ds(i * run, run)], sems.at[first + i]
        )
        for i in range(count)
    ]


def load_kernel(first, source, after, target, done, sems):
    done[...] = jnp.zeros_like(done)
    copies = pieces(source.at[pl.ds(first, target.shape[0])], target, sems, 0)
    for copy in copies:
        copy.start()
    for copy in copies:
        copy.wait()


def load(source, after, part=0, parts=1):
    rows = source.shape[0] // parts
    return pl.pallas_call(
        functools.partial(load_kernel, part * rows),
        out_shape=(
            VMEM_ARRAY((rows, source.shape[1]), source.dtype),
            VMEM_ARRAY((8, LANES), jnp.float32),
        ),
        in_specs=[IN_HBM, IN_VMEM],
        out_specs=(IN_VMEM, IN_VMEM),
        scratch_shapes=[pltpu.SemaphoreType.DMA((4,))],
        compiler_params=pltpu.CompilerParams(vmem_limit_bytes=MIB),
        cost_estimate=pl.CostEstimate(
            flops=0,
            bytes_accessed=2 * rows * source.shape[1] * source.dtype.itemsize,
            transcendentals=0,
        ),
    )(in_hbm(source), in_vmem(after))


def pass_on(kernel, ins, outs, *refs):
    more = len(refs) - ins - outs
    kernel(*refs[:ins], *refs[ins + more // 2 : ins + more // 2 + outs])


def small_call(kernel, operands, shapes, carried, limit):
    ins, outs = len(operands), len(shapes)
    results = pl.pallas_call(
        functools.partial(pass_on, kernel, ins, outs),
        out_shape=tuple(shapes) + tuple(VMEM_ARRAY(c.shape, c.dtype) for c in carried),
        in_specs=[IN_VMEM] * ins + [ANYWHERE] * len(carried),
        out_specs=(IN_VMEM,) * outs + (ANYWHERE,) * len(carried),
        input_output_aliases={ins + i: outs + i for i in range(len(carried))},
        compiler_params=pltpu.CompilerParams(vmem_limit_bytes=limit),
    )(*operands, *[in_vmem(c) for c in carried])
    return results[:outs], tuple(results[outs:])


def attend_kernel(
    order, lengths_hbm, me, queries_hbm, cache, value_up, kept, sent, value_in, lengths, queries, held, wide, sems
):
    rows_dev, _, heads = queries.shape
    context = cache.shape[2]
    latent = wide.shape[-1]
    caches = [pltpu.make_async_copy(cache.at[r], held.at[r], sems.at[r]) for r in range(rows_dev)]
    first = [
        pltpu.make_async_copy(lengths_hbm, lengths, sems.at[rows_dev]),
        pltpu.make_async_copy(queries_hbm, queries, sems.at[rows_dev + 1]),
    ]
    weights = pltpu.make_async_copy(value_up, value_in, sems.at[rows_dev + 2])
    for copy in first + caches + [weights]:
        copy.start()
    for copy in first:
        copy.wait()
    for r in range(rows_dev):
        caches[r].wait()
        scores = score_scale * lax.dot_general(
            queries[r], held[r], (((0,), (0,)), ((), ())), preferred_element_type=jnp.float32
        )
        positions = lax.broadcasted_iota(jnp.int32, (heads, context), 1)
        scores = jnp.where(positions < lengths[r], scores, -jnp.inf)
        exp_scores = jnp.exp(scores - jnp.max(scores, axis=1, keepdims=True))
        inverse = 1.0 / jnp.sum(exp_scores, axis=1, keepdims=True)
        soft_weights = (exp_scores * inverse).astype(jnp.bfloat16)
        got = lax.dot_general(
            soft_weights,
            held[r, :latent],
            (((1,), (1,)), ((), ())),
            preferred_element_type=jnp.float32,
        )
        if order:
            per = wide.shape[1] // rows_dev
            wide[:, r * per : (r + 1) * per] = got.reshape(-1, per, latent)
        else:
            kept[r] = got.astype(kept.dtype)
    half = len(order) // 2
    for p, s in enumerate(order):
        target = (kept, sent)[p // half]
        target[p % half] = wide[me[0] ^ s].astype(target.dtype)
    weights.wait()


def attend(queries, latent_cache, cache_lengths, value_up, order, me):
    rows_dev, heads, key_width = queries.shape
    context = latent_cache.shape[1]
    heads_dev, latent, _ = value_up.shape
    shape = (len(order) // 2, rows_dev * heads_dev, latent) if order else (rows_dev, heads, latent)
    wide = (max(2 * shape[0], 1), shape[1], latent) if order else (1, 8, latent)
    spare = shape if order else (1, 16, latent)
    return pl.pallas_call(
        functools.partial(attend_kernel, order),
        out_shape=(
            VMEM_ARRAY(shape, jnp.bfloat16),
            VMEM_ARRAY(spare, jnp.bfloat16),
            VMEM_ARRAY(value_up.shape, value_up.dtype),
        ),
        in_specs=[IN_HBM, IN_SMEM, IN_HBM, IN_HBM, IN_HBM],
        out_specs=(IN_VMEM,) * 3,
        scratch_shapes=[
            pltpu.SMEM((rows_dev,), jnp.int32),
            pltpu.VMEM((rows_dev, key_width, heads), jnp.bfloat16),
            pltpu.VMEM((rows_dev, key_width, context), jnp.bfloat16),
            pltpu.VMEM(wide, jnp.float32),
            pltpu.SemaphoreType.DMA((rows_dev + 3,)),
        ],
        compiler_params=pltpu.CompilerParams(vmem_limit_bytes=24 * MIB),
    )(
        in_hbm(cache_lengths),
        me[None],
        in_hbm(queries.transpose(0, 2, 1)),
        in_hbm(latent_cache.transpose(0, 2, 1)),
        in_hbm(value_up),
    )


def dealt(sources, ways, run):
    return [
        [
            (a, (g * ways + i) * run)
            for a, blocks in enumerate(sources)
            for g in range(blocks // (ways * run))
        ]
        for i in range(ways)
    ]


def deal_kernel(plan, run, count, *refs):
    sources, targets = refs[:count], refs[-len(plan) :]
    for target, runs in zip(targets, plan):
        for j, (a, first) in enumerate(runs):
            target[j * run : (j + 1) * run] = sources[a][first : first + run]


def deal(sources, ways, run, waits_for=()):
    plan = dealt([a.shape[0] for a in sources], ways, run)
    shape = (len(plan[0]) * run, *sources[0].shape[1:])
    return pl.pallas_call(
        functools.partial(deal_kernel, plan, run, len(sources)),
        out_shape=tuple(jax.ShapeDtypeStruct(shape, sources[0].dtype) for _ in plan),
        in_specs=[IN_VMEM] * (len(sources) + len(waits_for)),
        out_specs=(IN_VMEM,) * ways,
        compiler_params=pltpu.CompilerParams(vmem_limit_bytes=4 * MIB),
    )(*sources, *waits_for)


def project_kernel(tile, count, *refs):
    row_of, value_up, top, bottom, hidden, tail = refs[count : count + 6]
    next_hbm, kept, sent, next_in, sems = refs[count + 6 :] if len(refs) > count + 8 else (
        None, *refs[count + 6 :], None, None
    )
    copies = pieces(next_hbm, next_in, sems, 0) if sems is not None else []
    for copy in copies:
        copy.start()
    heads_dev = value_up.shape[0]
    half, wide = kept.shape
    rows_dev, width = hidden.shape
    maps = jnp.concatenate([value_up[h] for h in range(heads_dev)], axis=1)
    by_head = jnp.concatenate([a[...].reshape(-1, a.shape[-1]) for a in refs[:count]], axis=0)
    mixed = jnp.dot(by_head, maps, preferred_element_type=jnp.float32)
    row_head = lax.rem(lax.broadcasted_iota(jnp.int32, mixed.shape, 0), heads_dev)
    value_dim = value_up.shape[2]
    column_head = lax.broadcasted_iota(jnp.int32, mixed.shape, 1) // value_dim
    mixed = jnp.where(row_head == column_head, mixed, 0.0).astype(jnp.bfloat16)
    source = lax.broadcasted_iota(jnp.int32, (2 * half, mixed.shape[0]), 1) // heads_dev
    select = (row_of[...] == source).astype(jnp.bfloat16)
    head_rows = jnp.dot(select, mixed, preferred_element_type=jnp.float32)
    head_rows = head_rows.astype(jnp.bfloat16)
    cut = top.shape[0]

    @pl.loop(0, width // tile)
    def _(i):
        columns = pl.ds(pl.multiple_of(i * tile, tile), tile)
        terms = jnp.dot(head_rows[:, :cut], top[:, columns], preferred_element_type=jnp.float32)
        terms += jnp.dot(
            head_rows[:, cut:], bottom[:, columns], preferred_element_type=jnp.float32
        )
        kept[:, columns] = terms[:half]
        kept[0:rows_dev, columns] += hidden[:, columns].astype(jnp.float32)
        sent[:, columns] = terms[half:].astype(sent.dtype)

    kept[:, width:] = jnp.zeros((half, wide - width), kept.dtype)
    kept[0:rows_dev, width:] = tail[...]
    sent[:, width:] = jnp.zeros((half, wide - width), sent.dtype)
    for copy in copies:
        copy.wait()


def project(by_head, row_of, value_up, top, bottom, hidden, tail, following):
    rows_in = row_of.shape[0]
    width = hidden.shape[1]
    shape = (rows_in // 2, width + LANES)
    results = pl.pallas_call(
        functools.partial(project_kernel, 512, len(by_head)),
        out_shape=(
            jax.ShapeDtypeStruct(shape, jnp.float32),
            jax.ShapeDtypeStruct(shape, jnp.bfloat16),
            *[VMEM_ARRAY(w.shape, w.dtype) for w in following],
        ),
        in_specs=[IN_VMEM] * (len(by_head) + 6) + [IN_HBM] * len(following),
        out_specs=(IN_VMEM,) * (2 + len(following)),
        scratch_shapes=[pltpu.SemaphoreType.DMA((4,))] * len(following),
        compiler_params=pltpu.CompilerParams(vmem_limit_bytes=8 * MIB),
    )(
        *by_head,
        row_of,
        in_vmem(value_up),
        in_vmem(top),
        in_vmem(bottom),
        hidden,
        tail,
        *[in_hbm(w) for w in following],
    )
    return results[:2], tuple(results[2:])


def halve_kernel(kept, got, next_kept, sent):
    half = sent.shape[0]
    total = kept[...] + got[...].astype(jnp.float32)
    next_kept[...] = total[:half]
    sent[...] = total[half:].astype(sent.dtype)


def swap_kernel(shift, kept, got, total_ref, sent):
    total = kept[...] + got[...].astype(jnp.float32)
    rows = total.shape[0]
    row = lax.broadcasted_iota(jnp.int32, total.shape, 0)
    later, earlier = pltpu.roll(total, rows - shift, 0), pltpu.roll(total, shift, 0)
    total_ref[...] = total
    sent[...] = jnp.where((row & shift) == 0, later, earlier).astype(sent.dtype)


def combine(kernel, kept, got, out_rows, carried=()):
    shape = (out_rows, kept.shape[1])
    shapes = (jax.ShapeDtypeStruct(shape, jnp.float32), jax.ShapeDtypeStruct(shape, jnp.bfloat16))
    return small_call(kernel, (kept, got), shapes, carried, 2 * MIB + 24 * kept.size)


def norm_kernel(kept, got, gain, residual, moe_in):
    rows_dev, width = residual.shape
    total = kept[...] + got[...].astype(jnp.float32)
    body = total[:, :width]
    square = jnp.mean(body * body, axis=1, keepdims=True)
    residual[...] = body[:rows_dev]
    moe_in[:, :width] = (body * lax.rsqrt(square + norm_eps) * gain[...]).astype(moe_in.dtype)
    moe_in[:, width:] = total[:, width:].astype(moe_in.dtype)


def norm(kept, got, gain, rows_dev, carried):
    shapes = (
        jax.ShapeDtypeStruct((rows_dev, gain.shape[1]), jnp.float32),
        jax.ShapeDtypeStruct(kept.shape, jnp.bfloat16),
    )
    return small_call(norm_kernel, (kept, got, gain), shapes, carried, 2 * MIB + 24 * kept.size)


def stack_kernel(first, second, out):
    rows = first.shape[0]
    out[:rows] = first[...]
    out[rows:] = second[...]


def stack(first, second, carried):
    shape = jax.ShapeDtypeStruct((2 * first.shape[0], first.shape[1]), first.dtype)
    (out,), carried = small_call(
        stack_kernel, (first, second), (shape,), carried, 2 * MIB + 8 * first.size
    )
    return out, carried


def strips(source, target, sems):
    count = sems.shape[0]
    run = source.shape[1] // count
    return [
        pltpu.make_async_copy(
            source.at[:, pl.ds(i * run, run)], target.at[:, pl.ds(i * run, run)], sems.at[i]
        )
        for i in range(count)
    ]


def expert_kernel(
    me, first, second, gate, up, down, kept, sent, moe_in, gates, units, up_in, down_in, up_sems, down_sems
):
    width, inner = gate.shape
    half = kept.shape[0]
    ups, downs = strips(up, up_in, up_sems), strips(down, down_in, down_sems)
    for copy in ups:
        copy.start()
    moe_in[:half] = first[...]
    moe_in[half:] = second[...]
    rows = moe_in[:, :width]
    strip = inner // len(ups)
    tail = moe_in[:, width:].astype(jnp.float32)
    column = lax.broadcasted_iota(jnp.int32, tail.shape, 1)
    expert = lax.rem(me[0], EXPERTS)
    mine = (column == expert) | (column == expert + EXPERTS)
    weight = jnp.sum(jnp.where(mine, tail, 0.0), axis=1, keepdims=True)

    @pl.loop(0, len(ups))
    def _(i):
        columns = pl.ds(pl.multiple_of(i * strip, strip), strip)
        gate_act = jnp.dot(rows, gate[:, columns], preferred_element_type=jnp.float32)
        gates[:, columns] = jax.nn.silu(gate_act)

    later = iter(downs)
    for i, copy in enumerate(ups):
        copy.wait()
        next(later).start()
        columns = slice(i * strip, (i + 1) * strip)
        up_act = jnp.dot(rows, up_in[:, columns], preferred_element_type=jnp.float32)
        units[:, columns] = (gates[:, columns] * up_act).astype(units.dtype)
    strip = width // len(downs)
    for i, copy in enumerate(downs):
        copy.wait()
        for ahead in later:
            ahead.start()
            break
        columns = slice(i * strip, (i + 1) * strip)
        terms = weight * jnp.dot(
            units[...], down_in[:, columns], preferred_element_type=jnp.float32
        )
        kept[:, columns] = terms[:half]
        sent[:, columns] = terms[half:].astype(sent.dtype)


def run_expert(me, first, second, gate, up, down):
    rows = 2 * first.shape[0]
    width, inner = gate.shape
    shape = (rows // 2, width)
    return pl.pallas_call(
        expert_kernel,
        out_shape=(
            jax.ShapeDtypeStruct(shape, jnp.float32),
            jax.ShapeDtypeStruct(shape, jnp.bfloat16),
        ),
        in_specs=[IN_SMEM] + [IN_VMEM] * 3 + [IN_HBM] * 2,
        out_specs=(IN_VMEM, IN_VMEM),
        scratch_shapes=[
            pltpu.VMEM((rows, first.shape[1]), jnp.bfloat16),
            pltpu.VMEM((rows, inner), jnp.float32),
            pltpu.VMEM((rows, inner), jnp.bfloat16),
            pltpu.VMEM(up.shape, up.dtype),
            pltpu.VMEM(down.shape, down.dtype),
            pltpu.SemaphoreType.DMA((4,)),
            pltpu.SemaphoreType.DMA((7,)),
        ],
        compiler_params=pltpu.CompilerParams(
            vmem_limit_bytes=4 * MIB + 4 * width * inner + 64 * rows * inner
        ),
    )(me, first, second, in_vmem(gate), in_hbm(up), in_hbm(down))


def on_device(
    hidden,
    queries,
    latent_cache,
    cache_lengths,
    value_up,
    out_proj,
    norm_gain,
    expert_ids,
    gate_weights,
    gate_proj,
    up_proj,
    down_proj,
):
    rows_dev, width = hidden.shape
    ep_size = lax.axis_size("ep")
    me = lax.axis_index("ep")
    bits = ep_size.bit_length() - 1
    split_ways = ep_size // EXPERTS
    scatter_bits = min(2, bits)
    heads_dev, latent, _ = value_up.shape
    rows_in = ep_size * rows_dev

    experts_iota = lax.broadcasted_iota(jnp.int32, (1, 1, EXPERTS), 2)
    named = expert_ids[:, :, None] == experts_iota
    weight = jnp.sum(jnp.where(named, gate_weights[:, :, None], 0.0), axis=1)
    weight_top = weight.astype(jnp.bfloat16).astype(jnp.float32)
    weight_rest = (weight - weight_top).astype(jnp.bfloat16).astype(jnp.float32)
    tail = jnp.concatenate((weight_top, weight_rest), axis=1)
    tail = jnp.pad(tail, ((0, 0), (0, LANES - tail.shape[1])))

    order = relative_order(bits)
    gate, up, down = gate_proj[0], up_proj[0], down_proj[0]
    if heads_dev % 8 == 0:
        kept, sent, value_up = attend(queries, latent_cache, cache_lengths, value_up, order, me)
        run = ep_size >> 2
        got = exchange(sent, 0)
        kept, sent = deal((kept, got), 2, run)
        got = exchange(sent, 1)
        top, token = load(out_proj, sent, 0, 2)
        parts = deal((kept, got), run, 1, (token,))
        bottom, _ = load(out_proj, parts[0], 1, 2)
        masks = order[:run]
        by_head = [parts[0]] + [trade(part, mask) for part, mask in zip(parts[1:], masks[1:])]
        held = [mask | x << 1 | core for mask in masks for x in range(2) for core in range(2)]
        row_of = jnp.array([held.index(s) * rows_dev + r for s in order for r in range(rows_dev)])
    else:
        out, _, value_up = attend(queries, latent_cache, cache_lengths, value_up, (), me)
        top, _ = load(out_proj, value_up, 0, 2)
        bottom, _ = load(out_proj, value_up, 1, 2)
        out = out.reshape(rows_dev, ep_size, heads_dev, latent).transpose(1, 0, 2, 3)
        by_head = [lax.all_to_all(out, "ep", split_axis=0, concat_axis=0, tiled=True)]
        by_head = [by_head[0].reshape(rows_in * heads_dev, latent)]
        row_of = (jnp.array(order) ^ me)[:, None] * rows_dev + jnp.arange(rows_dev)[None, :]
        row_of = row_of.reshape(-1)
    row_of = row_of.astype(jnp.int32)
    following = (gate,) if split_ways == 1 else ()
    (kept, sent), carried = project(
        by_head, row_of[:, None], value_up, top, bottom, hidden, tail, following
    )

    rows = rows_in // 2
    for bit in range(scatter_bits - 1):
        rows //= 2
        (kept, sent), carried = combine(
            halve_kernel, kept, exchange(sent, bit), rows, carried
        )
    got = exchange(sent, scatter_bits - 1)
    for bit in range(scatter_bits, bits):
        swap = functools.partial(swap_kernel, rows_dev << (bits - 1 - bit))
        (kept, sent), carried = combine(swap, kept, got, rows, carried)
        got = exchange(sent, bit)
    (residual, moe_in), carried = norm(kept, got, norm_gain[None, :], rows_dev, carried)
    for bit in reversed(range(1, scatter_bits)):
        moe_in, carried = stack(moe_in, exchange(moe_in, bit), carried)
    other = exchange(moe_in, 0)

    if split_ways == 1:
        kept, sent = run_expert(me[None], moe_in, other, carried[0], up, down)
    else:
        moe_in = jnp.concatenate((moe_in, other), axis=0)
        expert = me % EXPERTS
        tail_in = moe_in[:, width:].astype(jnp.float32)
        column = lax.broadcasted_iota(jnp.int32, tail_in.shape, 1)
        mine = (column == expert) | (column == expert + EXPERTS)
        row_weight = jnp.sum(jnp.where(mine, tail_in, 0.0), axis=1, keepdims=True)
        slice_width = width // split_ways
        start = (me // EXPERTS) * slice_width
        part_in = lax.dynamic_slice_in_dim(moe_in, start, slice_width, axis=1)
        gate_act = jnp.dot(part_in, gate, preferred_element_type=jnp.float32)
        up_act = jnp.dot(part_in, up, preferred_element_type=jnp.float32)
        to_one = (row_of[:, None] == jnp.arange(rows_in)[None, :]).astype(jnp.float32)
        stacked = jnp.stack((gate_act, up_act)).astype(jnp.bfloat16).astype(jnp.float32)
        stacked = jnp.einsum("sr,asf->arf", to_one, stacked)
        for bit in range(EXPERTS.bit_length() - 1, bits):
            stacked = stacked + exchange(stacked.astype(jnp.bfloat16), bit).astype(jnp.float32)
        stacked = jnp.einsum("sr,arf->asf", to_one, stacked, precision=lax.Precision.HIGHEST)
        units = (jax.nn.silu(stacked[0]) * stacked[1]).astype(jnp.bfloat16)
        weighted = jnp.dot(units, down, preferred_element_type=jnp.float32) * row_weight
        spread = jnp.zeros((rows_in, width), jnp.float32)
        spread = lax.dynamic_update_slice_in_dim(spread, weighted, start, axis=1)
        kept, sent = spread[: rows_in // 2], spread[rows_in // 2 :].astype(jnp.bfloat16)
    rows = rows_in // 2
    for bit in range(bits - 1):
        rows //= 2
        (kept, sent), _ = combine(halve_kernel, kept, exchange(sent, bit), rows)
    routed = kept + exchange(sent, bits - 1).astype(jnp.float32)
    return (residual + routed).astype(jnp.bfloat16)


def solution(mesh):
    return jax.shard_map(
        on_device,
        mesh=mesh,
        in_specs=(
            P(("groups", "ep"), None),
            P(("groups", "ep"), None, None),
            P(("groups", "ep"), None, None),
            P(("groups", "ep")),
            P("ep", None, None),
            P("ep", None),
            P(),
            P(("groups", "ep"), None),
            P(("groups", "ep"), None),
            P("ep", None, None),
            P("ep", None, None),
            P("ep", None, None),
        ),
        out_specs=P(("groups", "ep"), None),
        check_vma=False,
    )
```

```python
import functools

import jax
import jax.numpy as jnp
from jax import lax
from jax.experimental import pallas as pl
from jax.experimental.pallas import tpu as pltpu
from jax.sharding import PartitionSpec as P

EXPERTS = 16


score_scale = 0.07216878364870323
norm_eps = 1e-06


def exchange(value, bit):
    return trade(value, 1 << bit)


def trade(value, mask):
    return lax.ppermute(value, "ep", [(i, i ^ mask) for i in range(lax.axis_size("ep"))])


def relative_order(bits):
    return [sum(((p >> (bits - 1 - b)) & 1) << b for b in range(bits)) for p in range(1 << bits)]


LANES = 128
MIB = 1 << 20
IN_VMEM = pl.BlockSpec(memory_space=pltpu.VMEM)
IN_SMEM = pl.BlockSpec(memory_space=pltpu.SMEM)
IN_HBM = pl.BlockSpec(memory_space=pltpu.HBM)
VMEM_ARRAY = pltpu.VMEM


def in_vmem(value):
    return pltpu.with_memory_space_constraint(value, pltpu.VMEM)


def in_hbm(value):
    return pltpu.with_memory_space_constraint(value, pltpu.HBM)


def pieces(source, target, sems, first):
    count = sems.shape[0] - first
    run = source.shape[0] // count
    return [
        pltpu.make_async_copy(
            source.at[pl.ds(i * run, run)], target.at[pl.ds(i * run, run)], sems.at[first + i]
        )
        for i in range(count)
    ]


def load_kernel(first, source, after, target, done, sems):
    done[...] = jnp.zeros_like(done)
    copies = pieces(source.at[pl.ds(first, target.shape[0])], target, sems, 0)
    for copy in copies:
        copy.start()
    for copy in copies:
        copy.wait()


def load(source, after, limit, part, parts=2):
    rows = source.shape[0] // parts
    return pl.pallas_call(
        functools.partial(load_kernel, part * rows),
        out_shape=(
            VMEM_ARRAY((rows, source.shape[1]), source.dtype),
            VMEM_ARRAY((8, LANES), jnp.float32),
        ),
        in_specs=[IN_HBM, IN_VMEM],
        out_specs=(IN_VMEM, IN_VMEM),
        scratch_shapes=[pltpu.SemaphoreType.DMA((4,))],
        compiler_params=pltpu.CompilerParams(vmem_limit_bytes=limit),
        cost_estimate=pl.CostEstimate(
            flops=0,
            bytes_accessed=2 * rows * source.shape[1] * source.dtype.itemsize,
            transcendentals=0,
        ),
    )(in_hbm(source), in_vmem(after))


def grant(rows, columns):
    return 4 * MIB + 16 * rows * columns


def only(kernel, ins, outs, *refs):
    kernel(*refs[:ins], *refs[len(refs) - outs :])


def small_call(kernel, operands, shapes, waits_for, limit):
    ins, outs = len(operands), len(shapes)
    return pl.pallas_call(
        functools.partial(only, kernel, ins, outs),
        out_shape=tuple(shapes),
        in_specs=[IN_VMEM] * (ins + len(waits_for)),
        out_specs=(IN_VMEM,) * outs,
        compiler_params=pltpu.CompilerParams(vmem_limit_bytes=limit),
    )(*operands, *waits_for)


def attend_kernel(
    order, lengths_hbm, me, queries_hbm, cache, value_up, kept, sent, value_in, lengths, queries, held, wide, sems
):
    rows_dev, _, heads = queries.shape
    context = cache.shape[2]
    latent = wide.shape[-1]
    caches = [pltpu.make_async_copy(cache.at[r], held.at[r], sems.at[r]) for r in range(rows_dev)]
    first = [
        pltpu.make_async_copy(lengths_hbm, lengths, sems.at[rows_dev]),
        pltpu.make_async_copy(queries_hbm, queries, sems.at[rows_dev + 1]),
    ]
    weights = pltpu.make_async_copy(value_up, value_in, sems.at[rows_dev + 2])
    for copy in first + caches + [weights]:
        copy.start()
    for copy in first:
        copy.wait()
    for r in range(rows_dev):
        caches[r].wait()
        scores = score_scale * lax.dot_general(
            queries[r], held[r], (((0,), (0,)), ((), ())), preferred_element_type=jnp.float32
        )
        positions = lax.broadcasted_iota(jnp.int32, (heads, context), 1)
        scores = jnp.where(positions < lengths[r], scores, -jnp.inf)
        exp_scores = jnp.exp(scores - jnp.max(scores, axis=1, keepdims=True))
        inverse = 1.0 / jnp.sum(exp_scores, axis=1, keepdims=True)
        soft_weights = (exp_scores * inverse).astype(jnp.bfloat16)
        got = lax.dot_general(
            soft_weights,
            held[r, :latent],
            (((1,), (1,)), ((), ())),
            preferred_element_type=jnp.float32,
        )
        if order:
            per = wide.shape[1] // rows_dev
            wide[:, r * per : (r + 1) * per] = got.reshape(-1, per, latent)
        else:
            kept[r] = got.astype(kept.dtype)
    half = len(order) // 2
    for p, s in enumerate(order):
        target = (kept, sent)[p // half]
        target[p % half] = wide[me[0] ^ s].astype(target.dtype)
    weights.wait()


def attend(queries, latent_cache, cache_lengths, value_up, order, me):
    rows_dev, heads, key_width = queries.shape
    context = latent_cache.shape[1]
    heads_dev, latent, _ = value_up.shape
    shape = (len(order) // 2, rows_dev * heads_dev, latent) if order else (rows_dev, heads, latent)
    wide = (max(2 * shape[0], 1), shape[1], latent) if order else (1, 8, latent)
    spare = shape if order else (1, 16, latent)
    return pl.pallas_call(
        functools.partial(attend_kernel, order),
        out_shape=(
            VMEM_ARRAY(shape, jnp.bfloat16),
            VMEM_ARRAY(spare, jnp.bfloat16),
            VMEM_ARRAY(value_up.shape, value_up.dtype),
        ),
        in_specs=[IN_HBM, IN_SMEM, IN_HBM, IN_HBM, IN_HBM],
        out_specs=(IN_VMEM,) * 3,
        scratch_shapes=[
            pltpu.SMEM((rows_dev,), jnp.int32),
            pltpu.VMEM((rows_dev, key_width, heads), jnp.bfloat16),
            pltpu.VMEM((rows_dev, key_width, context), jnp.bfloat16),
            pltpu.VMEM(wide, jnp.float32),
            pltpu.SemaphoreType.DMA((rows_dev + 3,)),
        ],
        compiler_params=pltpu.CompilerParams(vmem_limit_bytes=24 * MIB),
    )(
        in_hbm(cache_lengths),
        me[None],
        in_hbm(queries.transpose(0, 2, 1)),
        in_hbm(latent_cache.transpose(0, 2, 1)),
        in_hbm(value_up),
    )


def dealt(sources, ways, run):
    return [
        [
            (a, (g * ways + i) * run)
            for a, blocks in enumerate(sources)
            for g in range(blocks // (ways * run))
        ]
        for i in range(ways)
    ]


def deal_kernel(plan, run, count, *refs):
    sources, targets = refs[:count], refs[-len(plan) :]
    for target, runs in zip(targets, plan):
        for j, (a, first) in enumerate(runs):
            target[j * run : (j + 1) * run] = sources[a][first : first + run]


def deal(sources, ways, run, limit, waits_for=()):
    plan = dealt([a.shape[0] for a in sources], ways, run)
    shape = (len(plan[0]) * run, *sources[0].shape[1:])
    return pl.pallas_call(
        functools.partial(deal_kernel, plan, run, len(sources)),
        out_shape=tuple(jax.ShapeDtypeStruct(shape, sources[0].dtype) for _ in plan),
        in_specs=[IN_VMEM] * (len(sources) + len(waits_for)),
        out_specs=(IN_VMEM,) * ways,
        compiler_params=pltpu.CompilerParams(vmem_limit_bytes=limit),
    )(*sources, *waits_for)


def project_kernel(tile, count, *refs):
    row_of, value_up, top, bottom, hidden, tail = refs[count : count + 6]
    next_hbm, kept, sent, next_in, sems = refs[count + 6 :] if len(refs) > count + 8 else (
        None, *refs[count + 6 :], None, None
    )
    copies = []
    if sems is not None:
        copies = pieces(next_hbm.at[pl.ds(0, next_in.shape[0])], next_in, sems, 0)
    for copy in copies:
        copy.start()
    heads_dev = value_up.shape[0]
    half, wide = kept.shape
    rows_dev, width = hidden.shape
    maps = jnp.concatenate([value_up[h] for h in range(heads_dev)], axis=1)
    by_head = jnp.concatenate([a[...].reshape(-1, a.shape[-1]) for a in refs[:count]], axis=0)
    mixed = jnp.dot(by_head, maps, preferred_element_type=jnp.float32)
    row_head = lax.rem(lax.broadcasted_iota(jnp.int32, mixed.shape, 0), heads_dev)
    value_dim = value_up.shape[2]
    column_head = lax.broadcasted_iota(jnp.int32, mixed.shape, 1) // value_dim
    mixed = jnp.where(row_head == column_head, mixed, 0.0).astype(jnp.bfloat16)
    source = lax.broadcasted_iota(jnp.int32, (2 * half, mixed.shape[0]), 1) // heads_dev
    select = (row_of[...] == source).astype(jnp.bfloat16)
    head_rows = jnp.dot(select, mixed, preferred_element_type=jnp.float32)
    head_rows = head_rows.astype(jnp.bfloat16)
    cut = top.shape[0]

    @pl.loop(0, width // tile)
    def _(i):
        columns = pl.ds(pl.multiple_of(i * tile, tile), tile)
        terms = jnp.dot(head_rows[:, :cut], top[:, columns], preferred_element_type=jnp.float32)
        terms += jnp.dot(
            head_rows[:, cut:], bottom[:, columns], preferred_element_type=jnp.float32
        )
        kept[:, columns] = terms[:half]
        kept[0:rows_dev, columns] += hidden[:, columns].astype(jnp.float32)
        sent[:, columns] = terms[half:].astype(sent.dtype)

    kept[:, width:] = jnp.zeros((half, wide - width), kept.dtype)
    kept[0:rows_dev, width:] = tail[...]
    sent[:, width:] = jnp.zeros((half, wide - width), sent.dtype)
    for copy in copies:
        copy.wait()


def project(by_head, row_of, value_up, top, bottom, hidden, tail, following, limit):
    rows_in = row_of.shape[0]
    width = hidden.shape[1]
    shape = (rows_in // 2, width + LANES)
    results = pl.pallas_call(
        functools.partial(project_kernel, width // 2, len(by_head)),
        out_shape=(
            jax.ShapeDtypeStruct(shape, jnp.float32),
            jax.ShapeDtypeStruct(shape, jnp.bfloat16),
            *[VMEM_ARRAY((w.shape[0] // 2, w.shape[1]), w.dtype) for w in following],
        ),
        in_specs=[IN_VMEM] * (len(by_head) + 6) + [IN_HBM] * len(following),
        out_specs=(IN_VMEM,) * (2 + len(following)),
        scratch_shapes=[pltpu.SemaphoreType.DMA((4,))] * len(following),
        compiler_params=pltpu.CompilerParams(vmem_limit_bytes=limit),
    )(
        *by_head,
        row_of,
        in_vmem(value_up),
        in_vmem(top),
        in_vmem(bottom),
        hidden,
        tail,
        *[in_hbm(w) for w in following],
    )
    return results[:2], tuple(results[2:])


def halve_kernel(kept, got, next_kept, sent):
    half = sent.shape[0]
    total = kept[...] + got[...].astype(jnp.float32)
    next_kept[...] = total[:half]
    sent[...] = total[half:].astype(sent.dtype)


def swap_kernel(shift, kept, got, total_ref, sent):
    total = kept[...] + got[...].astype(jnp.float32)
    rows = total.shape[0]
    row = lax.broadcasted_iota(jnp.int32, total.shape, 0)
    later, earlier = pltpu.roll(total, rows - shift, 0), pltpu.roll(total, shift, 0)
    total_ref[...] = total
    sent[...] = jnp.where((row & shift) == 0, later, earlier).astype(sent.dtype)


def combine(kernel, kept, got, out_rows, limit, waits_for=()):
    shape = (out_rows, kept.shape[1])
    shapes = (jax.ShapeDtypeStruct(shape, jnp.float32), jax.ShapeDtypeStruct(shape, jnp.bfloat16))
    return small_call(kernel, (kept, got), shapes, waits_for, limit)


def norm_kernel(kept, got, gain, residual, moe_in):
    rows_dev, width = residual.shape
    total = kept[...] + got[...].astype(jnp.float32)
    body = total[:, :width]
    square = jnp.mean(body * body, axis=1, keepdims=True)
    residual[...] = body[:rows_dev]
    moe_in[:, :width] = (body * lax.rsqrt(square + norm_eps) * gain[...]).astype(moe_in.dtype)
    moe_in[:, width:] = total[:, width:].astype(moe_in.dtype)


def norm(kept, got, gain, rows_dev, limit, waits_for):
    shapes = (
        jax.ShapeDtypeStruct((rows_dev, gain.shape[1]), jnp.float32),
        jax.ShapeDtypeStruct(kept.shape, jnp.bfloat16),
    )
    return small_call(norm_kernel, (kept, got, gain), shapes, waits_for, limit)


def stack_kernel(first, second, out):
    rows = first.shape[0]
    out[:rows] = first[...]
    out[rows:] = second[...]


def stack(first, second, limit):
    shape = jax.ShapeDtypeStruct((2 * first.shape[0], first.shape[1]), first.dtype)
    return small_call(stack_kernel, (first, second), (shape,), (), limit)[0]


def strips(source, target, sems):
    count = sems.shape[0]
    run = source.shape[1] // count
    return [
        pltpu.make_async_copy(
            source.at[:, pl.ds(i * run, run)], target.at[:, pl.ds(i * run, run)], sems.at[i]
        )
        for i in range(count)
    ]


def expert_kernel(
    me, first, second, gate_top, gate_bottom, up_top, up_bottom, down, kept, sent, moe_in, units, down_in, sems
):
    cut, inner = gate_top.shape
    width = 2 * cut
    half = kept.shape[0]
    downs = strips(down, down_in, sems)
    for copy in downs:
        copy.start()
    moe_in[:half] = first[...]
    moe_in[half:] = second[...]
    tail = moe_in[:, width:].astype(jnp.float32)
    column = lax.broadcasted_iota(jnp.int32, tail.shape, 1)
    expert = lax.rem(me[0], EXPERTS)
    mine = (column == expert) | (column == expert + EXPERTS)
    weight = jnp.sum(jnp.where(mine, tail, 0.0), axis=1, keepdims=True)

    def product(top, bottom, columns):
        return jnp.dot(
            moe_in[:, :cut], top[:, columns], preferred_element_type=jnp.float32
        ) + jnp.dot(moe_in[:, cut:width], bottom[:, columns], preferred_element_type=jnp.float32)

    strip = inner // 2
    for i in range(2):
        columns = slice(i * strip, (i + 1) * strip)
        gate_act = product(gate_top, gate_bottom, columns)
        up_act = product(up_top, up_bottom, columns)
        units[:, columns] = (jax.nn.silu(gate_act) * up_act).astype(units.dtype)
    for copy in downs:
        copy.wait()
    for i in range(2):
        columns = slice(i * cut, (i + 1) * cut)
        terms = weight * jnp.dot(
            units[...], down_in[:, columns], preferred_element_type=jnp.float32
        )
        kept[:, columns] = terms[:half]
        sent[:, columns] = terms[half:].astype(sent.dtype)


def run_expert(me, first, second, gate, up, down, limit):
    rows = 2 * first.shape[0]
    inner, width = down.shape
    shape = (rows // 2, width)
    return pl.pallas_call(
        expert_kernel,
        out_shape=(
            jax.ShapeDtypeStruct(shape, jnp.float32),
            jax.ShapeDtypeStruct(shape, jnp.bfloat16),
        ),
        in_specs=[IN_SMEM] + [IN_VMEM] * 6 + [IN_HBM],
        out_specs=(IN_VMEM, IN_VMEM),
        scratch_shapes=[
            pltpu.VMEM((rows, first.shape[1]), jnp.bfloat16),
            pltpu.VMEM((rows, inner), jnp.bfloat16),
            pltpu.VMEM(down.shape, down.dtype),
            pltpu.SemaphoreType.DMA((4,)),
        ],
        compiler_params=pltpu.CompilerParams(vmem_limit_bytes=limit + 2 * down.size),
    )(me, first, second, *[in_vmem(w) for w in gate + up], in_hbm(down))


def on_device(
    hidden,
    queries,
    latent_cache,
    cache_lengths,
    value_up,
    out_proj,
    norm_gain,
    expert_ids,
    gate_weights,
    gate_proj,
    up_proj,
    down_proj,
):
    rows_dev, width = hidden.shape
    ep_size = lax.axis_size("ep")
    me = lax.axis_index("ep")
    bits = ep_size.bit_length() - 1
    split_ways = ep_size // EXPERTS
    scatter_bits = min(2, bits)
    heads_dev, latent, _ = value_up.shape
    rows_in = ep_size * rows_dev

    experts_iota = lax.broadcasted_iota(jnp.int32, (1, 1, EXPERTS), 2)
    named = expert_ids[:, :, None] == experts_iota
    weight = jnp.sum(jnp.where(named, gate_weights[:, :, None], 0.0), axis=1)
    weight_top = weight.astype(jnp.bfloat16).astype(jnp.float32)
    weight_rest = (weight - weight_top).astype(jnp.bfloat16).astype(jnp.float32)
    tail = jnp.concatenate((weight_top, weight_rest), axis=1)
    tail = jnp.pad(tail, ((0, 0), (0, LANES - tail.shape[1])))

    order = relative_order(bits)
    limit = grant(rows_in, width)
    gate, up, down = gate_proj[0], up_proj[0], down_proj[0]
    if heads_dev % 8 == 0:
        kept, sent, value_up = attend(queries, latent_cache, cache_lengths, value_up, order, me)
        run = ep_size >> 2
        got = exchange(sent, 0)
        kept, sent = deal((kept, got), 2, run, limit)
        got = exchange(sent, 1)
        top, token = load(out_proj, sent, limit, 0)
        parts = deal((kept, got), run, 1, limit, (token,))
        bottom, _ = load(out_proj, parts[0], limit, 1)
        masks = order[:run]
        by_head = [parts[0]] + [trade(part, mask) for part, mask in zip(parts[1:], masks[1:])]
        held = [mask | x << 1 | core for mask in masks for x in range(2) for core in range(2)]
        row_of = jnp.array([held.index(s) * rows_dev + r for s in order for r in range(rows_dev)])
    else:
        out, _, value_up = attend(queries, latent_cache, cache_lengths, value_up, (), me)
        top, _ = load(out_proj, value_up, limit, 0)
        bottom, _ = load(out_proj, value_up, limit, 1)
        out = out.reshape(rows_dev, ep_size, heads_dev, latent).transpose(1, 0, 2, 3)
        by_head = [lax.all_to_all(out, "ep", split_axis=0, concat_axis=0, tiled=True)]
        by_head = [by_head[0].reshape(rows_in * heads_dev, latent)]
        row_of = (jnp.array(order) ^ me)[:, None] * rows_dev + jnp.arange(rows_dev)[None, :]
        row_of = row_of.reshape(-1)
    row_of = row_of.astype(jnp.int32)
    following = (gate,) if split_ways == 1 else ()
    (kept, sent), halves = project(
        by_head, row_of[:, None], value_up, top, bottom, hidden, tail, following, limit
    )
    halves, later = list(halves), [(gate, 1), (up, 0), (up, 1)] if split_ways == 1 else []

    def beside(value):
        if not later:
            return ()
        source, part = later.pop(0)
        half, token = load(source, value, limit, part)
        halves.append(half)
        return (token,)


    rows = rows_in // 2
    for bit in range(scatter_bits - 1):
        rows //= 2
        kept, sent = combine(halve_kernel, kept, exchange(sent, bit), rows, limit)
    got = exchange(sent, scatter_bits - 1)
    for bit in range(scatter_bits, bits):
        swap = functools.partial(swap_kernel, rows_dev << (bits - 1 - bit))
        kept, sent = combine(swap, kept, got, rows, limit, beside(sent))
        got = exchange(sent, bit)
    residual, moe_in = norm(kept, got, norm_gain[None, :], rows_dev, limit, beside(sent))
    for bit in reversed(range(1, scatter_bits)):
        moe_in = stack(moe_in, exchange(moe_in, bit), limit)
    other = exchange(moe_in, 0)

    if split_ways == 1:
        while later:
            beside(moe_in)
        kept, sent = run_expert(me[None], moe_in, other, halves[:2], halves[2:], down, limit)
    else:
        moe_in = jnp.concatenate((moe_in, other), axis=0)
        expert = me % EXPERTS
        tail_in = moe_in[:, width:].astype(jnp.float32)
        column = lax.broadcasted_iota(jnp.int32, tail_in.shape, 1)
        mine = (column == expert) | (column == expert + EXPERTS)
        row_weight = jnp.sum(jnp.where(mine, tail_in, 0.0), axis=1, keepdims=True)
        slice_width = width // split_ways
        start = (me // EXPERTS) * slice_width
        part_in = lax.dynamic_slice_in_dim(moe_in, start, slice_width, axis=1)
        gate_act = jnp.dot(part_in, gate, preferred_element_type=jnp.float32)
        up_act = jnp.dot(part_in, up, preferred_element_type=jnp.float32)
        to_one = (row_of[:, None] == jnp.arange(rows_in)[None, :]).astype(jnp.float32)
        stacked = jnp.stack((gate_act, up_act)).astype(jnp.bfloat16).astype(jnp.float32)
        stacked = jnp.einsum("sr,asf->arf", to_one, stacked)
        for bit in range(EXPERTS.bit_length() - 1, bits):
            stacked = stacked + exchange(stacked.astype(jnp.bfloat16), bit).astype(jnp.float32)
        stacked = jnp.einsum("sr,arf->asf", to_one, stacked, precision=lax.Precision.HIGHEST)
        units = (jax.nn.silu(stacked[0]) * stacked[1]).astype(jnp.bfloat16)
        weighted = jnp.dot(units, down, preferred_element_type=jnp.float32) * row_weight
        spread = jnp.zeros((rows_in, width), jnp.float32)
        spread = lax.dynamic_update_slice_in_dim(spread, weighted, start, axis=1)
        kept, sent = spread[: rows_in // 2], spread[rows_in // 2 :].astype(jnp.bfloat16)
    rows = rows_in // 2
    for bit in range(bits - 1):
        rows //= 2
        kept, sent = combine(halve_kernel, kept, exchange(sent, bit), rows, limit)
    routed = kept + exchange(sent, bits - 1).astype(jnp.float32)
    return (residual + routed).astype(jnp.bfloat16)


def solution(mesh):
    return jax.shard_map(
        on_device,
        mesh=mesh,
        in_specs=(
            P(("groups", "ep"), None),
            P(("groups", "ep"), None, None),
            P(("groups", "ep"), None, None),
            P(("groups", "ep")),
            P("ep", None, None),
            P("ep", None),
            P(),
            P(("groups", "ep"), None),
            P(("groups", "ep"), None),
            P("ep", None, None),
            P("ep", None, None),
            P("ep", None, None),
        ),
        out_specs=P(("groups", "ep"), None),
        check_vma=False,
    )
```

```python
import functools

import jax
import jax.numpy as jnp
from jax import lax
from jax.experimental import pallas as pl
from jax.experimental.pallas import tpu as pltpu
from jax.sharding import PartitionSpec as P

EXPERTS = 16


score_scale = 0.07216878364870323
norm_eps = 1e-06


def exchange(value, bit):
    return trade(value, 1 << bit)


def trade(value, mask):
    return lax.ppermute(value, "ep", [(i, i ^ mask) for i in range(lax.axis_size("ep"))])


def relative_order(bits):
    return [sum(((p >> (bits - 1 - b)) & 1) << b for b in range(bits)) for p in range(1 << bits)]


LANES = 128
MIB = 1 << 20
IN_VMEM = pl.BlockSpec(memory_space=pltpu.VMEM)
IN_SMEM = pl.BlockSpec(memory_space=pltpu.SMEM)
IN_HBM = pl.BlockSpec(memory_space=pltpu.HBM)
VMEM_ARRAY = pltpu.VMEM


def in_vmem(value):
    return pltpu.with_memory_space_constraint(value, pltpu.VMEM)


def in_hbm(value):
    return pltpu.with_memory_space_constraint(value, pltpu.HBM)


def pieces(source, target, sems, first):
    count = sems.shape[0] - first
    run = source.shape[0] // count
    return [
        pltpu.make_async_copy(
            source.at[pl.ds(i * run, run)], target.at[pl.ds(i * run, run)], sems.at[first + i]
        )
        for i in range(count)
    ]


def load_kernel(first, source, after, target, done, sems):
    done[...] = jnp.zeros_like(done)
    copies = pieces(source.at[pl.ds(first, target.shape[0])], target, sems, 0)
    for copy in copies:
        copy.start()
    for copy in copies:
        copy.wait()


def load(source, after, limit, part, parts=2):
    rows = source.shape[0] // parts
    return pl.pallas_call(
        functools.partial(load_kernel, part * rows),
        out_shape=(
            VMEM_ARRAY((rows, source.shape[1]), source.dtype),
            VMEM_ARRAY((8, LANES), jnp.float32),
        ),
        in_specs=[IN_HBM, IN_VMEM],
        out_specs=(IN_VMEM, IN_VMEM),
        scratch_shapes=[pltpu.SemaphoreType.DMA((4,))],
        compiler_params=pltpu.CompilerParams(vmem_limit_bytes=limit),
        cost_estimate=pl.CostEstimate(
            flops=0,
            bytes_accessed=2 * rows * source.shape[1] * source.dtype.itemsize,
            transcendentals=0,
        ),
    )(in_hbm(source), in_vmem(after))


def grant(rows, columns):
    return 4 * MIB + 16 * rows * columns


def only(kernel, ins, outs, *refs):
    kernel(*refs[:ins], *refs[len(refs) - outs :])


def small_call(kernel, operands, shapes, waits_for, limit):
    ins, outs = len(operands), len(shapes)
    return pl.pallas_call(
        functools.partial(only, kernel, ins, outs),
        out_shape=tuple(shapes),
        in_specs=[IN_VMEM] * (ins + len(waits_for)),
        out_specs=(IN_VMEM,) * outs,
        compiler_params=pltpu.CompilerParams(vmem_limit_bytes=limit),
    )(*operands, *waits_for)


def attend_kernel(
    order, lengths_hbm, me, queries_hbm, cache, value_up, kept, sent, value_in, lengths, queries, held, wide, sems
):
    rows_dev, _, heads = queries.shape
    context = cache.shape[2]
    latent = wide.shape[-1]
    caches = [pltpu.make_async_copy(cache.at[r], held.at[r], sems.at[r]) for r in range(rows_dev)]
    first = [
        pltpu.make_async_copy(lengths_hbm, lengths, sems.at[rows_dev]),
        pltpu.make_async_copy(queries_hbm, queries, sems.at[rows_dev + 1]),
    ]
    weights = pltpu.make_async_copy(value_up, value_in, sems.at[rows_dev + 2])
    for copy in first + caches + [weights]:
        copy.start()
    for copy in first:
        copy.wait()
    for r in range(rows_dev):
        caches[r].wait()
        scores = score_scale * lax.dot_general(
            queries[r], held[r], (((0,), (0,)), ((), ())), preferred_element_type=jnp.float32
        )
        positions = lax.broadcasted_iota(jnp.int32, (heads, context), 1)
        scores = jnp.where(positions < lengths[r], scores, -jnp.inf)
        exp_scores = jnp.exp(scores - jnp.max(scores, axis=1, keepdims=True))
        inverse = 1.0 / jnp.sum(exp_scores, axis=1, keepdims=True)
        soft_weights = (exp_scores * inverse).astype(jnp.bfloat16)
        got = lax.dot_general(
            soft_weights,
            held[r, :latent],
            (((1,), (1,)), ((), ())),
            preferred_element_type=jnp.float32,
        )
        if order:
            per = wide.shape[1] // rows_dev
            wide[:, r * per : (r + 1) * per] = got.reshape(-1, per, latent)
        else:
            kept[r] = got.astype(kept.dtype)
    half = len(order) // 2
    for p, s in enumerate(order):
        target = (kept, sent)[p // half]
        target[p % half] = wide[me[0] ^ s].astype(target.dtype)
    weights.wait()


def attend(queries, latent_cache, cache_lengths, value_up, order, me):
    rows_dev, heads, key_width = queries.shape
    context = latent_cache.shape[1]
    heads_dev, latent, _ = value_up.shape
    shape = (len(order) // 2, rows_dev * heads_dev, latent) if order else (rows_dev, heads, latent)
    wide = (max(2 * shape[0], 1), shape[1], latent) if order else (1, 8, latent)
    spare = shape if order else (1, 16, latent)
    return pl.pallas_call(
        functools.partial(attend_kernel, order),
        out_shape=(
            VMEM_ARRAY(shape, jnp.bfloat16),
            VMEM_ARRAY(spare, jnp.bfloat16),
            VMEM_ARRAY(value_up.shape, value_up.dtype),
        ),
        in_specs=[IN_HBM, IN_SMEM, IN_HBM, IN_HBM, IN_HBM],
        out_specs=(IN_VMEM,) * 3,
        scratch_shapes=[
            pltpu.SMEM((rows_dev,), jnp.int32),
            pltpu.VMEM((rows_dev, key_width, heads), jnp.bfloat16),
            pltpu.VMEM((rows_dev, key_width, context), jnp.bfloat16),
            pltpu.VMEM(wide, jnp.float32),
            pltpu.SemaphoreType.DMA((rows_dev + 3,)),
        ],
        compiler_params=pltpu.CompilerParams(vmem_limit_bytes=24 * MIB),
    )(
        in_hbm(cache_lengths),
        me[None],
        in_hbm(queries.transpose(0, 2, 1)),
        in_hbm(latent_cache.transpose(0, 2, 1)),
        in_hbm(value_up),
    )


def dealt(sources, ways, run):
    return [
        [
            (a, (g * ways + i) * run)
            for a, blocks in enumerate(sources)
            for g in range(blocks // (ways * run))
        ]
        for i in range(ways)
    ]


def deal_kernel(plan, run, count, *refs):
    sources, targets = refs[:count], refs[-len(plan) :]
    for target, runs in zip(targets, plan):
        for j, (a, first) in enumerate(runs):
            target[j * run : (j + 1) * run] = sources[a][first : first + run]


def deal(sources, ways, run, limit, waits_for=()):
    plan = dealt([a.shape[0] for a in sources], ways, run)
    shape = (len(plan[0]) * run, *sources[0].shape[1:])
    return pl.pallas_call(
        functools.partial(deal_kernel, plan, run, len(sources)),
        out_shape=tuple(jax.ShapeDtypeStruct(shape, sources[0].dtype) for _ in plan),
        in_specs=[IN_VMEM] * (len(sources) + len(waits_for)),
        out_specs=(IN_VMEM,) * ways,
        compiler_params=pltpu.CompilerParams(vmem_limit_bytes=limit),
    )(*sources, *waits_for)


def project_kernel(tile, count, *refs):
    row_of, value_up, top, bottom, hidden, tail = refs[count : count + 6]
    next_hbm, kept, sent, next_in, sems = refs[count + 6 :] if len(refs) > count + 8 else (
        None, *refs[count + 6 :], None, None
    )
    copies = []
    if sems is not None:
        copies = pieces(next_hbm.at[pl.ds(0, next_in.shape[0])], next_in, sems, 0)
    for copy in copies:
        copy.start()
    heads_dev = value_up.shape[0]
    half, wide = kept.shape
    rows_dev, width = hidden.shape
    maps = jnp.concatenate([value_up[h] for h in range(heads_dev)], axis=1)
    by_head = jnp.concatenate([a[...].reshape(-1, a.shape[-1]) for a in refs[:count]], axis=0)
    mixed = jnp.dot(by_head, maps, preferred_element_type=jnp.float32)
    row_head = lax.rem(lax.broadcasted_iota(jnp.int32, mixed.shape, 0), heads_dev)
    value_dim = value_up.shape[2]
    column_head = lax.broadcasted_iota(jnp.int32, mixed.shape, 1) // value_dim
    mixed = jnp.where(row_head == column_head, mixed, 0.0).astype(jnp.bfloat16)
    source = lax.broadcasted_iota(jnp.int32, (2 * half, mixed.shape[0]), 1) // heads_dev
    select = (row_of[...] == source).astype(jnp.bfloat16)
    head_rows = jnp.dot(select, mixed, preferred_element_type=jnp.float32)
    head_rows = head_rows.astype(jnp.bfloat16)
    cut = top.shape[0]

    @pl.loop(0, width // tile)
    def _(i):
        columns = pl.ds(pl.multiple_of(i * tile, tile), tile)
        terms = jnp.dot(head_rows[:, :cut], top[:, columns], preferred_element_type=jnp.float32)
        terms += jnp.dot(
            head_rows[:, cut:], bottom[:, columns], preferred_element_type=jnp.float32
        )
        kept[:, columns] = terms[:half]
        kept[0:rows_dev, columns] += hidden[:, columns].astype(jnp.float32)
        sent[:, columns] = terms[half:].astype(sent.dtype)

    kept[:, width:] = jnp.zeros((half, wide - width), kept.dtype)
    kept[0:rows_dev, width:] = tail[...]
    sent[:, width:] = jnp.zeros((half, wide - width), sent.dtype)
    for copy in copies:
        copy.wait()


def project(by_head, row_of, value_up, top, bottom, hidden, tail, following, limit):
    rows_in = row_of.shape[0]
    width = hidden.shape[1]
    shape = (rows_in // 2, width + LANES)
    results = pl.pallas_call(
        functools.partial(project_kernel, width // 2, len(by_head)),
        out_shape=(
            jax.ShapeDtypeStruct(shape, jnp.float32),
            jax.ShapeDtypeStruct(shape, jnp.bfloat16),
            *[VMEM_ARRAY((w.shape[0] // 2, w.shape[1]), w.dtype) for w in following],
        ),
        in_specs=[IN_VMEM] * (len(by_head) + 6) + [IN_HBM] * len(following),
        out_specs=(IN_VMEM,) * (2 + len(following)),
        scratch_shapes=[pltpu.SemaphoreType.DMA((4,))] * len(following),
        compiler_params=pltpu.CompilerParams(vmem_limit_bytes=limit),
    )(
        *by_head,
        row_of,
        in_vmem(value_up),
        in_vmem(top),
        in_vmem(bottom),
        hidden,
        tail,
        *[in_hbm(w) for w in following],
    )
    return results[:2], tuple(results[2:])


def halve_kernel(kept, got, next_kept, sent):
    half = sent.shape[0]
    total = kept[...] + got[...].astype(jnp.float32)
    next_kept[...] = total[:half]
    sent[...] = total[half:].astype(sent.dtype)


def swap_kernel(shift, kept, got, total_ref, sent):
    total = kept[...] + got[...].astype(jnp.float32)
    rows = total.shape[0]
    row = lax.broadcasted_iota(jnp.int32, total.shape, 0)
    later, earlier = pltpu.roll(total, rows - shift, 0), pltpu.roll(total, shift, 0)
    total_ref[...] = total
    sent[...] = jnp.where((row & shift) == 0, later, earlier).astype(sent.dtype)


def combine(kernel, kept, got, out_rows, limit, waits_for=()):
    shape = (out_rows, kept.shape[1])
    shapes = (jax.ShapeDtypeStruct(shape, jnp.float32), jax.ShapeDtypeStruct(shape, jnp.bfloat16))
    return small_call(kernel, (kept, got), shapes, waits_for, limit)


def norm_kernel(kept, got, gain, residual, moe_in):
    rows_dev, width = residual.shape
    total = kept[...] + got[...].astype(jnp.float32)
    body = total[:, :width]
    square = jnp.mean(body * body, axis=1, keepdims=True)
    residual[...] = body[:rows_dev]
    moe_in[:, :width] = (body * lax.rsqrt(square + norm_eps) * gain[...]).astype(moe_in.dtype)
    moe_in[:, width:] = total[:, width:].astype(moe_in.dtype)


def norm(kept, got, gain, rows_dev, limit, waits_for):
    shapes = (
        jax.ShapeDtypeStruct((rows_dev, gain.shape[1]), jnp.float32),
        jax.ShapeDtypeStruct(kept.shape, jnp.bfloat16),
    )
    return small_call(norm_kernel, (kept, got, gain), shapes, waits_for, limit)


def stack_kernel(first, second, out):
    rows = first.shape[0]
    out[:rows] = first[...]
    out[rows:] = second[...]


def stack(first, second, limit):
    shape = jax.ShapeDtypeStruct((2 * first.shape[0], first.shape[1]), first.dtype)
    return small_call(stack_kernel, (first, second), (shape,), (), limit)[0]


def strips(source, target, sems):
    count = sems.shape[0]
    run = source.shape[1] // count
    return [
        pltpu.make_async_copy(
            source.at[:, pl.ds(i * run, run)], target.at[:, pl.ds(i * run, run)], sems.at[i]
        )
        for i in range(count)
    ]


def expert_kernel(
    me, first, second, gate_top, gate_bottom, up_top, up_bottom, down, kept, sent, moe_in, units, down_in, sems
):
    cut, inner = gate_top.shape
    width = 2 * cut
    half = kept.shape[0]
    downs = strips(down, down_in, sems)
    for copy in downs:
        copy.start()
    moe_in[:half] = first[...]
    moe_in[half:] = second[...]
    tail = moe_in[:, width:].astype(jnp.float32)
    column = lax.broadcasted_iota(jnp.int32, tail.shape, 1)
    expert = lax.rem(me[0], EXPERTS)
    mine = (column == expert) | (column == expert + EXPERTS)
    weight = jnp.sum(jnp.where(mine, tail, 0.0), axis=1, keepdims=True)

    def product(top, bottom, columns):
        return jnp.dot(
            moe_in[:, :cut], top[:, columns], preferred_element_type=jnp.float32
        ) + jnp.dot(moe_in[:, cut:width], bottom[:, columns], preferred_element_type=jnp.float32)

    strip = inner // 2

    @pl.loop(0, 2)
    def _(i):
        columns = pl.ds(pl.multiple_of(i * strip, strip), strip)
        gate_act = product(gate_top, gate_bottom, columns)
        up_act = product(up_top, up_bottom, columns)
        units[:, columns] = (jax.nn.silu(gate_act) * up_act).astype(units.dtype)
    for copy in downs:
        copy.wait()

    @pl.loop(0, 2)
    def _(i):
        columns = pl.ds(pl.multiple_of(i * cut, cut), cut)
        terms = weight * jnp.dot(
            units[...], down_in[:, columns], preferred_element_type=jnp.float32
        )
        kept[:, columns] = terms[:half]
        sent[:, columns] = terms[half:].astype(sent.dtype)


def run_expert(me, first, second, gate, up, down, limit):
    rows = 2 * first.shape[0]
    inner, width = down.shape
    shape = (rows // 2, width)
    return pl.pallas_call(
        expert_kernel,
        out_shape=(
            jax.ShapeDtypeStruct(shape, jnp.float32),
            jax.ShapeDtypeStruct(shape, jnp.bfloat16),
        ),
        in_specs=[IN_SMEM] + [IN_VMEM] * 6 + [IN_HBM],
        out_specs=(IN_VMEM, IN_VMEM),
        scratch_shapes=[
            pltpu.VMEM((rows, first.shape[1]), jnp.bfloat16),
            pltpu.VMEM((rows, inner), jnp.bfloat16),
            pltpu.VMEM(down.shape, down.dtype),
            pltpu.SemaphoreType.DMA((4,)),
        ],
        compiler_params=pltpu.CompilerParams(vmem_limit_bytes=limit + 2 * down.size),
    )(me, first, second, *[in_vmem(w) for w in gate + up], in_hbm(down))


def on_device(
    hidden,
    queries,
    latent_cache,
    cache_lengths,
    value_up,
    out_proj,
    norm_gain,
    expert_ids,
    gate_weights,
    gate_proj,
    up_proj,
    down_proj,
):
    rows_dev, width = hidden.shape
    ep_size = lax.axis_size("ep")
    me = lax.axis_index("ep")
    bits = ep_size.bit_length() - 1
    split_ways = ep_size // EXPERTS
    scatter_bits = min(2, bits)
    heads_dev, latent, _ = value_up.shape
    rows_in = ep_size * rows_dev

    experts_iota = lax.broadcasted_iota(jnp.int32, (1, 1, EXPERTS), 2)
    named = expert_ids[:, :, None] == experts_iota
    weight = jnp.sum(jnp.where(named, gate_weights[:, :, None], 0.0), axis=1)
    weight_top = weight.astype(jnp.bfloat16).astype(jnp.float32)
    weight_rest = (weight - weight_top).astype(jnp.bfloat16).astype(jnp.float32)
    tail = jnp.concatenate((weight_top, weight_rest), axis=1)
    tail = jnp.pad(tail, ((0, 0), (0, LANES - tail.shape[1])))

    order = relative_order(bits)
    limit = grant(rows_in, width)
    gate, up, down = gate_proj[0], up_proj[0], down_proj[0]
    if heads_dev % 8 == 0:
        kept, sent, value_up = attend(queries, latent_cache, cache_lengths, value_up, order, me)
        run = ep_size >> 2
        got = exchange(sent, 0)
        kept, sent = deal((kept, got), 2, run, limit)
        got = exchange(sent, 1)
        top, token = load(out_proj, sent, limit, 0)
        parts = deal((kept, got), run, 1, limit, (token,))
        bottom, _ = load(out_proj, parts[0], limit, 1)
        masks = order[:run]
        by_head = [parts[0]] + [trade(part, mask) for part, mask in zip(parts[1:], masks[1:])]
        held = [mask | x << 1 | core for mask in masks for x in range(2) for core in range(2)]
        row_of = jnp.array([held.index(s) * rows_dev + r for s in order for r in range(rows_dev)])
    else:
        out, _, value_up = attend(queries, latent_cache, cache_lengths, value_up, (), me)
        top, _ = load(out_proj, value_up, limit, 0)
        bottom, _ = load(out_proj, value_up, limit, 1)
        out = out.reshape(rows_dev, ep_size, heads_dev, latent).transpose(1, 0, 2, 3)
        by_head = [lax.all_to_all(out, "ep", split_axis=0, concat_axis=0, tiled=True)]
        by_head = [by_head[0].reshape(rows_in * heads_dev, latent)]
        row_of = (jnp.array(order) ^ me)[:, None] * rows_dev + jnp.arange(rows_dev)[None, :]
        row_of = row_of.reshape(-1)
    row_of = row_of.astype(jnp.int32)
    following = (gate,) if split_ways == 1 else ()
    (kept, sent), halves = project(
        by_head, row_of[:, None], value_up, top, bottom, hidden, tail, following, limit
    )
    halves, later = list(halves), [(gate, 1), (up, 0), (up, 1)] if split_ways == 1 else []

    def beside(value):
        if not later:
            return ()
        source, part = later.pop(0)
        half, token = load(source, value, limit, part)
        halves.append(half)
        return (token,)


    rows = rows_in // 2
    for bit in range(scatter_bits - 1):
        rows //= 2
        kept, sent = combine(halve_kernel, kept, exchange(sent, bit), rows, limit)
    got = exchange(sent, scatter_bits - 1)
    for bit in range(scatter_bits, bits):
        swap = functools.partial(swap_kernel, rows_dev << (bits - 1 - bit))
        kept, sent = combine(swap, kept, got, rows, limit, beside(sent))
        got = exchange(sent, bit)
    residual, moe_in = norm(kept, got, norm_gain[None, :], rows_dev, limit, beside(sent))
    for bit in reversed(range(1, scatter_bits)):
        moe_in = stack(moe_in, exchange(moe_in, bit), limit)
    other = exchange(moe_in, 0)

    if split_ways == 1:
        while later:
            beside(moe_in)
        kept, sent = run_expert(me[None], moe_in, other, halves[:2], halves[2:], down, limit)
    else:
        moe_in = jnp.concatenate((moe_in, other), axis=0)
        expert = me % EXPERTS
        tail_in = moe_in[:, width:].astype(jnp.float32)
        column = lax.broadcasted_iota(jnp.int32, tail_in.shape, 1)
        mine = (column == expert) | (column == expert + EXPERTS)
        row_weight = jnp.sum(jnp.where(mine, tail_in, 0.0), axis=1, keepdims=True)
        slice_width = width // split_ways
        start = (me // EXPERTS) * slice_width
        part_in = lax.dynamic_slice_in_dim(moe_in, start, slice_width, axis=1)
        gate_act = jnp.dot(part_in, gate, preferred_element_type=jnp.float32)
        up_act = jnp.dot(part_in, up, preferred_element_type=jnp.float32)
        to_one = (row_of[:, None] == jnp.arange(rows_in)[None, :]).astype(jnp.float32)
        stacked = jnp.stack((gate_act, up_act)).astype(jnp.bfloat16).astype(jnp.float32)
        stacked = jnp.einsum("sr,asf->arf", to_one, stacked)
        for bit in range(EXPERTS.bit_length() - 1, bits):
            stacked = stacked + exchange(stacked.astype(jnp.bfloat16), bit).astype(jnp.float32)
        stacked = jnp.einsum("sr,arf->asf", to_one, stacked, precision=lax.Precision.HIGHEST)
        units = (jax.nn.silu(stacked[0]) * stacked[1]).astype(jnp.bfloat16)
        weighted = jnp.dot(units, down, preferred_element_type=jnp.float32) * row_weight
        spread = jnp.zeros((rows_in, width), jnp.float32)
        spread = lax.dynamic_update_slice_in_dim(spread, weighted, start, axis=1)
        kept, sent = spread[: rows_in // 2], spread[rows_in // 2 :].astype(jnp.bfloat16)
    rows = rows_in // 2
    for bit in range(bits - 1):
        rows //= 2
        kept, sent = combine(halve_kernel, kept, exchange(sent, bit), rows, limit)
    routed = kept + exchange(sent, bits - 1).astype(jnp.float32)
    return (residual + routed).astype(jnp.bfloat16)


def solution(mesh):
    return jax.shard_map(
        on_device,
        mesh=mesh,
        in_specs=(
            P(("groups", "ep"), None),
            P(("groups", "ep"), None, None),
            P(("groups", "ep"), None, None),
            P(("groups", "ep")),
            P("ep", None, None),
            P("ep", None),
            P(),
            P(("groups", "ep"), None),
            P(("groups", "ep"), None),
            P("ep", None, None),
            P("ep", None, None),
            P("ep", None, None),
        ),
        out_specs=P(("groups", "ep"), None),
        check_vma=False,
    )
```

```python
import functools

import jax
import jax.numpy as jnp
from jax import lax
from jax.experimental import pallas as pl
from jax.experimental.pallas import tpu as pltpu
from jax.sharding import PartitionSpec as P

EXPERTS = 16


score_scale = 0.07216878364870323
norm_eps = 1e-06


def exchange(value, bit):
    return trade(value, 1 << bit)


def trade(value, mask):
    return lax.ppermute(value, "ep", [(i, i ^ mask) for i in range(lax.axis_size("ep"))])


def relative_order(bits):
    return [sum(((p >> (bits - 1 - b)) & 1) << b for b in range(bits)) for p in range(1 << bits)]


LANES = 128
MIB = 1 << 20
IN_VMEM = pl.BlockSpec(memory_space=pltpu.VMEM)
IN_HBM = pl.BlockSpec(memory_space=pltpu.HBM)
VMEM_ARRAY = pltpu.VMEM


def in_vmem(value):
    return pltpu.with_memory_space_constraint(value, pltpu.VMEM)


def in_hbm(value):
    return pltpu.with_memory_space_constraint(value, pltpu.HBM)


def pieces(source, target, sems, first):
    count = sems.shape[0] - first
    run = source.shape[0] // count
    return [
        pltpu.make_async_copy(
            source.at[pl.ds(i * run, run)], target.at[pl.ds(i * run, run)], sems.at[first + i]
        )
        for i in range(count)
    ]


def load_kernel(first, source, after, target, done, sems):
    done[...] = jnp.zeros_like(done)
    copies = pieces(source.at[pl.ds(first, target.shape[0])], target, sems, 0)
    for copy in copies:
        copy.start()
    for copy in copies:
        copy.wait()


def load(source, after, limit, part, parts=2):
    rows = source.shape[0] // parts
    return pl.pallas_call(
        functools.partial(load_kernel, part * rows),
        out_shape=(
            VMEM_ARRAY((rows, source.shape[1]), source.dtype),
            VMEM_ARRAY((8, LANES), jnp.float32),
        ),
        in_specs=[IN_HBM, IN_VMEM],
        out_specs=(IN_VMEM, IN_VMEM),
        scratch_shapes=[pltpu.SemaphoreType.DMA((4,))],
        compiler_params=pltpu.CompilerParams(vmem_limit_bytes=limit),
        cost_estimate=pl.CostEstimate(
            flops=0,
            bytes_accessed=2 * rows * source.shape[1] * source.dtype.itemsize,
            transcendentals=0,
        ),
    )(in_hbm(source), in_vmem(after))


def grant(rows, columns):
    return 4 * MIB + 16 * rows * columns


def only(kernel, ins, outs, *refs):
    kernel(*refs[:ins], *refs[len(refs) - outs :])


def small_call(kernel, operands, shapes, waits_for, limit):
    ins, outs = len(operands), len(shapes)
    return pl.pallas_call(
        functools.partial(only, kernel, ins, outs),
        out_shape=tuple(shapes),
        in_specs=[IN_VMEM] * (ins + len(waits_for)),
        out_specs=(IN_VMEM,) * outs,
        compiler_params=pltpu.CompilerParams(vmem_limit_bytes=limit),
    )(*operands, *waits_for)


def attend_kernel(
    order, lengths_hbm, queries_hbm, cache, value_up, kept, sent, value_in, lengths, queries, held, wide, sems
):
    rows_dev, _, heads = queries.shape
    context = cache.shape[2]
    latent = wide.shape[-1]
    caches = [pltpu.make_async_copy(cache.at[r], held.at[r], sems.at[r]) for r in range(rows_dev)]
    first = [
        pltpu.make_async_copy(lengths_hbm, lengths, sems.at[rows_dev]),
        pltpu.make_async_copy(queries_hbm, queries, sems.at[rows_dev + 1]),
    ]
    weights = pltpu.make_async_copy(value_up, value_in, sems.at[rows_dev + 2])
    for copy in first + caches + [weights]:
        copy.start()
    for copy in first:
        copy.wait()
    for r in range(rows_dev):
        caches[r].wait()
        scores = score_scale * lax.dot_general(
            queries[r], held[r], (((0,), (0,)), ((), ())), preferred_element_type=jnp.float32
        )
        positions = lax.broadcasted_iota(jnp.int32, (heads, context), 1)
        scores = jnp.where(positions < lengths[r], scores, -jnp.inf)
        exp_scores = jnp.exp(scores - jnp.max(scores, axis=1, keepdims=True))
        inverse = 1.0 / jnp.sum(exp_scores, axis=1, keepdims=True)
        soft_weights = (exp_scores * inverse).astype(jnp.bfloat16)
        got = lax.dot_general(
            soft_weights,
            held[r, :latent],
            (((1,), (1,)), ((), ())),
            preferred_element_type=jnp.float32,
        )
        if order:
            per = wide.shape[1] // rows_dev
            wide[:, r * per : (r + 1) * per] = got.reshape(-1, per, latent)
        else:
            kept[r] = got.astype(kept.dtype)
    half = len(order) // 2
    me = lax.axis_index("ep")
    for p, s in enumerate(order):
        target = (kept, sent)[p // half]
        target[p % half] = wide[me ^ s].astype(target.dtype)
    weights.wait()


def attend(queries, latent_cache, cache_lengths, value_up, order):
    rows_dev, heads, key_width = queries.shape
    context = latent_cache.shape[1]
    heads_dev, latent, _ = value_up.shape
    shape = (len(order) // 2, rows_dev * heads_dev, latent) if order else (rows_dev, heads, latent)
    wide = (max(2 * shape[0], 1), shape[1], latent) if order else (1, 8, latent)
    spare = shape if order else (1, 16, latent)
    return pl.pallas_call(
        functools.partial(attend_kernel, order),
        out_shape=(
            VMEM_ARRAY(shape, jnp.bfloat16),
            VMEM_ARRAY(spare, jnp.bfloat16),
            VMEM_ARRAY(value_up.shape, value_up.dtype),
        ),
        in_specs=[IN_HBM] * 4,
        out_specs=(IN_VMEM,) * 3,
        scratch_shapes=[
            pltpu.SMEM((rows_dev,), jnp.int32),
            pltpu.VMEM((rows_dev, key_width, heads), jnp.bfloat16),
            pltpu.VMEM((rows_dev, key_width, context), jnp.bfloat16),
            pltpu.VMEM(wide, jnp.float32),
            pltpu.SemaphoreType.DMA((rows_dev + 3,)),
        ],
        compiler_params=pltpu.CompilerParams(vmem_limit_bytes=24 * MIB),
    )(
        in_hbm(cache_lengths),
        in_hbm(queries.transpose(0, 2, 1)),
        in_hbm(latent_cache.transpose(0, 2, 1)),
        in_hbm(value_up),
    )


def dealt(sources, ways, run):
    return [
        [
            (a, (g * ways + i) * run)
            for a, blocks in enumerate(sources)
            for g in range(blocks // (ways * run))
        ]
        for i in range(ways)
    ]


def deal_kernel(plan, run, count, *refs):
    sources, targets = refs[:count], refs[-len(plan) :]
    for target, runs in zip(targets, plan):
        for j, (a, first) in enumerate(runs):
            target[j * run : (j + 1) * run] = sources[a][first : first + run]


def deal(sources, ways, run, limit, waits_for=()):
    plan = dealt([a.shape[0] for a in sources], ways, run)
    shape = (len(plan[0]) * run, *sources[0].shape[1:])
    return pl.pallas_call(
        functools.partial(deal_kernel, plan, run, len(sources)),
        out_shape=tuple(jax.ShapeDtypeStruct(shape, sources[0].dtype) for _ in plan),
        in_specs=[IN_VMEM] * (len(sources) + len(waits_for)),
        out_specs=(IN_VMEM,) * ways,
        compiler_params=pltpu.CompilerParams(vmem_limit_bytes=limit),
    )(*sources, *waits_for)


def project_kernel(tile, count, *refs):
    row_of, value_up, top, bottom, hidden, tail = refs[count : count + 6]
    next_hbm, kept, sent, next_in, sems = refs[count + 6 :] if len(refs) > count + 8 else (
        None, *refs[count + 6 :], None, None
    )
    copies = []
    if sems is not None:
        copies = pieces(next_hbm.at[pl.ds(0, next_in.shape[0])], next_in, sems, 0)
    for copy in copies:
        copy.start()
    heads_dev = value_up.shape[0]
    half, wide = kept.shape
    rows_dev, width = hidden.shape
    maps = jnp.concatenate([value_up[h] for h in range(heads_dev)], axis=1)
    by_head = jnp.concatenate([a[...].reshape(-1, a.shape[-1]) for a in refs[:count]], axis=0)
    mixed = jnp.dot(by_head, maps, preferred_element_type=jnp.float32)
    row_head = lax.rem(lax.broadcasted_iota(jnp.int32, mixed.shape, 0), heads_dev)
    value_dim = value_up.shape[2]
    column_head = lax.broadcasted_iota(jnp.int32, mixed.shape, 1) // value_dim
    mixed = jnp.where(row_head == column_head, mixed, 0.0).astype(jnp.bfloat16)
    source = lax.broadcasted_iota(jnp.int32, (2 * half, mixed.shape[0]), 1) // heads_dev
    select = (row_of[...] == source).astype(jnp.bfloat16)
    head_rows = jnp.dot(select, mixed, preferred_element_type=jnp.float32)
    head_rows = head_rows.astype(jnp.bfloat16)
    cut = top.shape[0]

    @pl.loop(0, width // tile)
    def _(i):
        columns = pl.ds(pl.multiple_of(i * tile, tile), tile)
        terms = jnp.dot(head_rows[:, :cut], top[:, columns], preferred_element_type=jnp.float32)
        terms += jnp.dot(
            head_rows[:, cut:], bottom[:, columns], preferred_element_type=jnp.float32
        )
        kept[:, columns] = terms[:half]
        kept[0:rows_dev, columns] += hidden[:, columns].astype(jnp.float32)
        sent[:, columns] = terms[half:].astype(sent.dtype)

    kept[:, width:] = jnp.zeros((half, wide - width), kept.dtype)
    kept[0:rows_dev, width:] = tail[...]
    sent[:, width:] = jnp.zeros((half, wide - width), sent.dtype)
    for copy in copies:
        copy.wait()


def project(by_head, row_of, value_up, top, bottom, hidden, tail, following, limit):
    rows_in = row_of.shape[0]
    width = hidden.shape[1]
    shape = (rows_in // 2, width + LANES)
    results = pl.pallas_call(
        functools.partial(project_kernel, width // 2, len(by_head)),
        out_shape=(
            jax.ShapeDtypeStruct(shape, jnp.float32),
            jax.ShapeDtypeStruct(shape, jnp.bfloat16),
            *[VMEM_ARRAY((w.shape[0] // 2, w.shape[1]), w.dtype) for w in following],
        ),
        in_specs=[IN_VMEM] * (len(by_head) + 6) + [IN_HBM] * len(following),
        out_specs=(IN_VMEM,) * (2 + len(following)),
        scratch_shapes=[pltpu.SemaphoreType.DMA((4,))] * len(following),
        compiler_params=pltpu.CompilerParams(vmem_limit_bytes=limit),
    )(
        *by_head,
        row_of,
        in_vmem(value_up),
        in_vmem(top),
        in_vmem(bottom),
        hidden,
        tail,
        *[in_hbm(w) for w in following],
    )
    return results[:2], tuple(results[2:])


def halve_kernel(kept, got, next_kept, sent):
    half = sent.shape[0]
    total = kept[...] + got[...].astype(jnp.float32)
    next_kept[...] = total[:half]
    sent[...] = total[half:].astype(sent.dtype)


def swap_kernel(shift, kept, got, total_ref, sent):
    total = kept[...] + got[...].astype(jnp.float32)
    rows = total.shape[0]
    row = lax.broadcasted_iota(jnp.int32, total.shape, 0)
    later, earlier = pltpu.roll(total, rows - shift, 0), pltpu.roll(total, shift, 0)
    total_ref[...] = total
    sent[...] = jnp.where((row & shift) == 0, later, earlier).astype(sent.dtype)


def combine(kernel, kept, got, out_rows, limit, waits_for=()):
    shape = (out_rows, kept.shape[1])
    shapes = (jax.ShapeDtypeStruct(shape, jnp.float32), jax.ShapeDtypeStruct(shape, jnp.bfloat16))
    return small_call(kernel, (kept, got), shapes, waits_for, limit)


def norm_kernel(kept, got, gain, residual, moe_in):
    rows_dev, width = residual.shape
    total = kept[...] + got[...].astype(jnp.float32)
    body = total[:, :width]
    square = jnp.mean(body * body, axis=1, keepdims=True)
    residual[...] = body[:rows_dev]
    moe_in[:, :width] = (body * lax.rsqrt(square + norm_eps) * gain[...]).astype(moe_in.dtype)
    moe_in[:, width:] = total[:, width:].astype(moe_in.dtype)


def norm(kept, got, gain, rows_dev, limit, waits_for):
    shapes = (
        jax.ShapeDtypeStruct((rows_dev, gain.shape[1]), jnp.float32),
        jax.ShapeDtypeStruct(kept.shape, jnp.bfloat16),
    )
    return small_call(norm_kernel, (kept, got, gain), shapes, waits_for, limit)


def stack_kernel(first, second, out):
    rows = first.shape[0]
    out[:rows] = first[...]
    out[rows:] = second[...]


def stack(first, second, limit):
    shape = jax.ShapeDtypeStruct((2 * first.shape[0], first.shape[1]), first.dtype)
    return small_call(stack_kernel, (first, second), (shape,), (), limit)[0]


def strips(source, target, sems):
    count = sems.shape[0]
    run = source.shape[1] // count
    return [
        pltpu.make_async_copy(
            source.at[:, pl.ds(i * run, run)], target.at[:, pl.ds(i * run, run)], sems.at[i]
        )
        for i in range(count)
    ]


def expert_kernel(
    first, second, gate_top, gate_bottom, up_top, up_bottom, down, kept, sent, moe_in, units, down_in, sems
):
    cut, inner = gate_top.shape
    width = 2 * cut
    half = kept.shape[0]
    downs = strips(down, down_in, sems)
    for copy in downs:
        copy.start()
    moe_in[:half] = first[...]
    moe_in[half:] = second[...]
    tail = moe_in[:, width:].astype(jnp.float32)
    column = lax.broadcasted_iota(jnp.int32, tail.shape, 1)
    expert = lax.rem(lax.axis_index("ep"), EXPERTS)
    mine = (column == expert) | (column == expert + EXPERTS)
    weight = jnp.sum(jnp.where(mine, tail, 0.0), axis=1, keepdims=True)

    def product(top, bottom, columns):
        return jnp.dot(
            moe_in[:, :cut], top[:, columns], preferred_element_type=jnp.float32
        ) + jnp.dot(moe_in[:, cut:width], bottom[:, columns], preferred_element_type=jnp.float32)

    strip = inner // 2

    @pl.loop(0, 2)
    def _(i):
        columns = pl.ds(pl.multiple_of(i * strip, strip), strip)
        gate_act = product(gate_top, gate_bottom, columns)
        up_act = product(up_top, up_bottom, columns)
        units[:, columns] = (jax.nn.silu(gate_act) * up_act).astype(units.dtype)
    for copy in downs:
        copy.wait()

    @pl.loop(0, 2)
    def _(i):
        columns = pl.ds(pl.multiple_of(i * cut, cut), cut)
        terms = weight * jnp.dot(
            units[...], down_in[:, columns], preferred_element_type=jnp.float32
        )
        kept[:, columns] = terms[:half]
        sent[:, columns] = terms[half:].astype(sent.dtype)


def run_expert(first, second, gate, up, down, limit):
    rows = 2 * first.shape[0]
    inner, width = down.shape
    shape = (rows // 2, width)
    return pl.pallas_call(
        expert_kernel,
        out_shape=(
            jax.ShapeDtypeStruct(shape, jnp.float32),
            jax.ShapeDtypeStruct(shape, jnp.bfloat16),
        ),
        in_specs=[IN_VMEM] * 6 + [IN_HBM],
        out_specs=(IN_VMEM, IN_VMEM),
        scratch_shapes=[
            pltpu.VMEM((rows, first.shape[1]), jnp.bfloat16),
            pltpu.VMEM((rows, inner), jnp.bfloat16),
            pltpu.VMEM(down.shape, down.dtype),
            pltpu.SemaphoreType.DMA((4,)),
        ],
        compiler_params=pltpu.CompilerParams(vmem_limit_bytes=limit + 2 * down.size),
    )(first, second, *[in_vmem(w) for w in gate + up], in_hbm(down))


def on_device(
    hidden,
    queries,
    latent_cache,
    cache_lengths,
    value_up,
    out_proj,
    norm_gain,
    expert_ids,
    gate_weights,
    gate_proj,
    up_proj,
    down_proj,
):
    rows_dev, width = hidden.shape
    ep_size = lax.axis_size("ep")
    me = lax.axis_index("ep")
    bits = ep_size.bit_length() - 1
    split_ways = ep_size // EXPERTS
    scatter_bits = min(2, bits)
    heads_dev, latent, _ = value_up.shape
    rows_in = ep_size * rows_dev

    experts_iota = lax.broadcasted_iota(jnp.int32, (1, 1, EXPERTS), 2)
    named = expert_ids[:, :, None] == experts_iota
    weight = jnp.sum(jnp.where(named, gate_weights[:, :, None], 0.0), axis=1)
    weight_top = weight.astype(jnp.bfloat16).astype(jnp.float32)
    weight_rest = (weight - weight_top).astype(jnp.bfloat16).astype(jnp.float32)
    tail = jnp.concatenate((weight_top, weight_rest), axis=1)
    tail = jnp.pad(tail, ((0, 0), (0, LANES - tail.shape[1])))

    order = relative_order(bits)
    limit = grant(rows_in, width)
    gate, up, down = gate_proj[0], up_proj[0], down_proj[0]
    if heads_dev % 8 == 0:
        kept, sent, value_up = attend(queries, latent_cache, cache_lengths, value_up, order)
        run = ep_size >> 2
        got = exchange(sent, 0)
        kept, sent = deal((kept, got), 2, run, limit)
        got = exchange(sent, 1)
        top, token = load(out_proj, sent, limit, 0)
        parts = deal((kept, got), run, 1, limit, (token,))
        bottom, _ = load(out_proj, parts[0], limit, 1)
        masks = order[:run]
        by_head = [parts[0]] + [trade(part, mask) for part, mask in zip(parts[1:], masks[1:])]
        held = [mask | x << 1 | core for mask in masks for x in range(2) for core in range(2)]
        row_of = jnp.array([held.index(s) * rows_dev + r for s in order for r in range(rows_dev)])
    else:
        out, _, value_up = attend(queries, latent_cache, cache_lengths, value_up, ())
        top, _ = load(out_proj, value_up, limit, 0)
        bottom, _ = load(out_proj, value_up, limit, 1)
        out = out.reshape(rows_dev, ep_size, heads_dev, latent).transpose(1, 0, 2, 3)
        by_head = [lax.all_to_all(out, "ep", split_axis=0, concat_axis=0, tiled=True)]
        by_head = [by_head[0].reshape(rows_in * heads_dev, latent)]
        row_of = (jnp.array(order) ^ me)[:, None] * rows_dev + jnp.arange(rows_dev)[None, :]
        row_of = row_of.reshape(-1)
    row_of = row_of.astype(jnp.int32)
    following = (gate,) if split_ways == 1 else ()
    (kept, sent), halves = project(
        by_head, row_of[:, None], value_up, top, bottom, hidden, tail, following, limit
    )
    halves, later = list(halves), [(gate, 1), (up, 0), (up, 1)] if split_ways == 1 else []

    def beside(value):
        if not later:
            return ()
        source, part = later.pop(0)
        half, token = load(source, value, limit, part)
        halves.append(half)
        return (token,)


    rows = rows_in // 2
    for bit in range(scatter_bits - 1):
        rows //= 2
        kept, sent = combine(halve_kernel, kept, exchange(sent, bit), rows, limit)
    got = exchange(sent, scatter_bits - 1)
    for bit in range(scatter_bits, bits):
        swap = functools.partial(swap_kernel, rows_dev << (bits - 1 - bit))
        kept, sent = combine(swap, kept, got, rows, limit, beside(sent))
        got = exchange(sent, bit)
    residual, moe_in = norm(kept, got, norm_gain[None, :], rows_dev, limit, beside(sent))
    for bit in reversed(range(1, scatter_bits)):
        moe_in = stack(moe_in, exchange(moe_in, bit), limit)
    other = exchange(moe_in, 0)

    if split_ways == 1:
        while later:
            beside(moe_in)
        kept, sent = run_expert(moe_in, other, halves[:2], halves[2:], down, limit)
    else:
        moe_in = jnp.concatenate((moe_in, other), axis=0)
        expert = me % EXPERTS
        tail_in = moe_in[:, width:].astype(jnp.float32)
        column = lax.broadcasted_iota(jnp.int32, tail_in.shape, 1)
        mine = (column == expert) | (column == expert + EXPERTS)
        row_weight = jnp.sum(jnp.where(mine, tail_in, 0.0), axis=1, keepdims=True)
        slice_width = width // split_ways
        start = (me // EXPERTS) * slice_width
        part_in = lax.dynamic_slice_in_dim(moe_in, start, slice_width, axis=1)
        gate_act = jnp.dot(part_in, gate, preferred_element_type=jnp.float32)
        up_act = jnp.dot(part_in, up, preferred_element_type=jnp.float32)
        to_one = (row_of[:, None] == jnp.arange(rows_in)[None, :]).astype(jnp.float32)
        stacked = jnp.stack((gate_act, up_act)).astype(jnp.bfloat16).astype(jnp.float32)
        stacked = jnp.einsum("sr,asf->arf", to_one, stacked)
        for bit in range(EXPERTS.bit_length() - 1, bits):
            stacked = stacked + exchange(stacked.astype(jnp.bfloat16), bit).astype(jnp.float32)
        stacked = jnp.einsum("sr,arf->asf", to_one, stacked, precision=lax.Precision.HIGHEST)
        units = (jax.nn.silu(stacked[0]) * stacked[1]).astype(jnp.bfloat16)
        weighted = jnp.dot(units, down, preferred_element_type=jnp.float32) * row_weight
        spread = jnp.zeros((rows_in, width), jnp.float32)
        spread = lax.dynamic_update_slice_in_dim(spread, weighted, start, axis=1)
        kept, sent = spread[: rows_in // 2], spread[rows_in // 2 :].astype(jnp.bfloat16)
    rows = rows_in // 2
    for bit in range(bits - 1):
        rows //= 2
        kept, sent = combine(halve_kernel, kept, exchange(sent, bit), rows, limit)
    routed = kept + exchange(sent, bits - 1).astype(jnp.float32)
    return (residual + routed).astype(jnp.bfloat16)


def solution(mesh):
    return jax.shard_map(
        on_device,
        mesh=mesh,
        in_specs=(
            P(("groups", "ep"), None),
            P(("groups", "ep"), None, None),
            P(("groups", "ep"), None, None),
            P(("groups", "ep")),
            P("ep", None, None),
            P("ep", None),
            P(),
            P(("groups", "ep"), None),
            P(("groups", "ep"), None),
            P("ep", None, None),
            P("ep", None, None),
            P("ep", None, None),
        ),
        out_specs=P(("groups", "ep"), None),
        check_vma=False,
    )
```

```python
import functools

import jax
import jax.numpy as jnp
from jax import lax
from jax.experimental import pallas as pl
from jax.experimental.pallas import tpu as pltpu
from jax.sharding import PartitionSpec as P

EXPERTS = 16


score_scale = 0.07216878364870323
norm_eps = 1e-06


def exchange(value, bit):
    return trade(value, 1 << bit)


def trade(value, mask):
    return lax.ppermute(value, "ep", [(i, i ^ mask) for i in range(lax.axis_size("ep"))])


def relative_order(bits):
    return [sum(((p >> (bits - 1 - b)) & 1) << b for b in range(bits)) for p in range(1 << bits)]


LANES = 128
MIB = 1 << 20
IN_VMEM = pl.BlockSpec(memory_space=pltpu.VMEM)
IN_SMEM = pl.BlockSpec(memory_space=pltpu.SMEM)
IN_HBM = pl.BlockSpec(memory_space=pltpu.HBM)
VMEM_ARRAY = pltpu.VMEM


def in_vmem(value):
    return pltpu.with_memory_space_constraint(value, pltpu.VMEM)


def in_hbm(value):
    return pltpu.with_memory_space_constraint(value, pltpu.HBM)


def pieces(source, target, sems, first):
    count = sems.shape[0] - first
    run = source.shape[0] // count
    return [
        pltpu.make_async_copy(
            source.at[pl.ds(i * run, run)], target.at[pl.ds(i * run, run)], sems.at[first + i]
        )
        for i in range(count)
    ]


def load_kernel(first, source, after, target, done, sems):
    done[...] = jnp.zeros_like(done)
    copies = pieces(source.at[pl.ds(first, target.shape[0])], target, sems, 0)
    for copy in copies:
        copy.start()
    for copy in copies:
        copy.wait()


def load(source, after, limit, part, parts=2):
    rows = source.shape[0] // parts
    return pl.pallas_call(
        functools.partial(load_kernel, part * rows),
        out_shape=(
            VMEM_ARRAY((rows, source.shape[1]), source.dtype),
            VMEM_ARRAY((8, LANES), jnp.float32),
        ),
        in_specs=[IN_HBM, IN_VMEM],
        out_specs=(IN_VMEM, IN_VMEM),
        scratch_shapes=[pltpu.SemaphoreType.DMA((4,))],
        compiler_params=pltpu.CompilerParams(vmem_limit_bytes=limit),
        cost_estimate=pl.CostEstimate(
            flops=0,
            bytes_accessed=2 * rows * source.shape[1] * source.dtype.itemsize,
            transcendentals=0,
        ),
    )(in_hbm(source), in_vmem(after))


def grant(rows, columns):
    return 4 * MIB + 16 * rows * columns


def only(kernel, ins, outs, *refs):
    kernel(*refs[:ins], *refs[len(refs) - outs :])


def small_call(kernel, operands, shapes, waits_for, limit):
    ins, outs = len(operands), len(shapes)
    return pl.pallas_call(
        functools.partial(only, kernel, ins, outs),
        out_shape=tuple(shapes),
        in_specs=[IN_VMEM] * (ins + len(waits_for)),
        out_specs=(IN_VMEM,) * outs,
        compiler_params=pltpu.CompilerParams(vmem_limit_bytes=limit),
    )(*operands, *waits_for)


def attend_kernel(
    order, lengths_hbm, me, queries_hbm, cache, value_up, kept, sent, value_in, lengths, queries, held, wide, sems
):
    rows_dev, _, heads = queries.shape
    context = cache.shape[2]
    latent = wide.shape[-1]
    caches = [pltpu.make_async_copy(cache.at[r], held.at[r], sems.at[r]) for r in range(rows_dev)]
    first = [
        pltpu.make_async_copy(lengths_hbm, lengths, sems.at[rows_dev]),
        pltpu.make_async_copy(queries_hbm, queries, sems.at[rows_dev + 1]),
    ]
    weights = pltpu.make_async_copy(value_up, value_in, sems.at[rows_dev + 2])
    for copy in first + caches + [weights]:
        copy.start()
    for copy in first:
        copy.wait()
    for r in range(rows_dev):
        caches[r].wait()
        scores = score_scale * lax.dot_general(
            queries[r], held[r], (((0,), (0,)), ((), ())), preferred_element_type=jnp.float32
        )
        positions = lax.broadcasted_iota(jnp.int32, (heads, context), 1)
        scores = jnp.where(positions < lengths[r], scores, -jnp.inf)
        exp_scores = jnp.exp(scores - jnp.max(scores, axis=1, keepdims=True))
        inverse = 1.0 / jnp.sum(exp_scores, axis=1, keepdims=True)
        soft_weights = (exp_scores * inverse).astype(jnp.bfloat16)
        got = lax.dot_general(
            soft_weights,
            held[r, :latent],
            (((1,), (1,)), ((), ())),
            preferred_element_type=jnp.float32,
        )
        if order:
            per = wide.shape[1] // rows_dev
            wide[:, r * per : (r + 1) * per] = got.reshape(-1, per, latent)
        else:
            kept[r] = got.astype(kept.dtype)
    half = len(order) // 2
    for p, s in enumerate(order):
        target = (kept, sent)[p // half]
        target[p % half] = wide[me[0] ^ s].astype(target.dtype)
    weights.wait()


def attend(queries, latent_cache, cache_lengths, value_up, order, me):
    rows_dev, heads, key_width = queries.shape
    context = latent_cache.shape[1]
    heads_dev, latent, _ = value_up.shape
    shape = (len(order) // 2, rows_dev * heads_dev, latent) if order else (rows_dev, heads, latent)
    wide = (max(2 * shape[0], 1), shape[1], latent) if order else (1, 8, latent)
    spare = shape if order else (1, 16, latent)
    return pl.pallas_call(
        functools.partial(attend_kernel, order),
        out_shape=(
            VMEM_ARRAY(shape, jnp.bfloat16),
            VMEM_ARRAY(spare, jnp.bfloat16),
            VMEM_ARRAY(value_up.shape, value_up.dtype),
        ),
        in_specs=[IN_HBM, IN_SMEM, IN_HBM, IN_HBM, IN_HBM],
        out_specs=(IN_VMEM,) * 3,
        scratch_shapes=[
            pltpu.SMEM((rows_dev,), jnp.int32),
            pltpu.VMEM((rows_dev, key_width, heads), jnp.bfloat16),
            pltpu.VMEM((rows_dev, key_width, context), jnp.bfloat16),
            pltpu.VMEM(wide, jnp.float32),
            pltpu.SemaphoreType.DMA((rows_dev + 3,)),
        ],
        compiler_params=pltpu.CompilerParams(vmem_limit_bytes=24 * MIB),
    )(
        in_hbm(cache_lengths),
        me[None],
        in_hbm(queries.transpose(0, 2, 1)),
        in_hbm(latent_cache.transpose(0, 2, 1)),
        in_hbm(value_up),
    )


def dealt(sources, ways, run):
    return [
        [
            (a, (g * ways + i) * run)
            for a, blocks in enumerate(sources)
            for g in range(blocks // (ways * run))
        ]
        for i in range(ways)
    ]


def deal_kernel(plan, run, count, *refs):
    sources, targets = refs[:count], refs[-len(plan) :]
    for target, runs in zip(targets, plan):
        for j, (a, first) in enumerate(runs):
            target[j * run : (j + 1) * run] = sources[a][first : first + run]


def deal(sources, ways, run, limit, waits_for=()):
    plan = dealt([a.shape[0] for a in sources], ways, run)
    shape = (len(plan[0]) * run, *sources[0].shape[1:])
    return pl.pallas_call(
        functools.partial(deal_kernel, plan, run, len(sources)),
        out_shape=tuple(jax.ShapeDtypeStruct(shape, sources[0].dtype) for _ in plan),
        in_specs=[IN_VMEM] * (len(sources) + len(waits_for)),
        out_specs=(IN_VMEM,) * ways,
        compiler_params=pltpu.CompilerParams(vmem_limit_bytes=limit),
    )(*sources, *waits_for)


def project_kernel(tile, count, *refs):
    row_of, value_up, top, bottom, hidden, tail, kept, sent = refs[count:]
    heads_dev = value_up.shape[0]
    half, wide = kept.shape
    rows_dev, width = hidden.shape
    maps = jnp.concatenate([value_up[h] for h in range(heads_dev)], axis=1)
    by_head = jnp.concatenate([a[...].reshape(-1, a.shape[-1]) for a in refs[:count]], axis=0)
    mixed = jnp.dot(by_head, maps, preferred_element_type=jnp.float32)
    row_head = lax.rem(lax.broadcasted_iota(jnp.int32, mixed.shape, 0), heads_dev)
    value_dim = value_up.shape[2]
    column_head = lax.broadcasted_iota(jnp.int32, mixed.shape, 1) // value_dim
    mixed = jnp.where(row_head == column_head, mixed, 0.0).astype(jnp.bfloat16)
    source = lax.broadcasted_iota(jnp.int32, (2 * half, mixed.shape[0]), 1) // heads_dev
    select = (row_of[...] == source).astype(jnp.bfloat16)
    head_rows = jnp.dot(select, mixed, preferred_element_type=jnp.float32)
    head_rows = head_rows.astype(jnp.bfloat16)
    cut = top.shape[0]

    @pl.loop(0, width // tile)
    def _(i):
        columns = pl.ds(pl.multiple_of(i * tile, tile), tile)
        terms = jnp.dot(head_rows[:, :cut], top[:, columns], preferred_element_type=jnp.float32)
        terms += jnp.dot(
            head_rows[:, cut:], bottom[:, columns], preferred_element_type=jnp.float32
        )
        kept[:, columns] = terms[:half]
        kept[0:rows_dev, columns] += hidden[:, columns].astype(jnp.float32)
        sent[:, columns] = terms[half:].astype(sent.dtype)

    kept[:, width:] = jnp.zeros((half, wide - width), kept.dtype)
    kept[0:rows_dev, width:] = tail[...]
    sent[:, width:] = jnp.zeros((half, wide - width), sent.dtype)


def project(by_head, row_of, value_up, top, bottom, hidden, tail, limit):
    rows_in = row_of.shape[0]
    width = hidden.shape[1]
    shape = (rows_in // 2, width + LANES)
    return pl.pallas_call(
        functools.partial(project_kernel, width // 2, len(by_head)),
        out_shape=(
            jax.ShapeDtypeStruct(shape, jnp.float32),
            jax.ShapeDtypeStruct(shape, jnp.bfloat16),
        ),
        in_specs=[IN_VMEM] * (len(by_head) + 6),
        out_specs=(IN_VMEM, IN_VMEM),
        compiler_params=pltpu.CompilerParams(vmem_limit_bytes=limit),
    )(
        *by_head,
        row_of,
        in_vmem(value_up),
        in_vmem(top),
        in_vmem(bottom),
        hidden,
        tail,
    )


def halve_kernel(kept, got, next_kept, sent):
    half = sent.shape[0]
    total = kept[...] + got[...].astype(jnp.float32)
    next_kept[...] = total[:half]
    sent[...] = total[half:].astype(sent.dtype)


def swap_kernel(shift, kept, got, total_ref, sent):
    total = kept[...] + got[...].astype(jnp.float32)
    rows = total.shape[0]
    row = lax.broadcasted_iota(jnp.int32, total.shape, 0)
    later, earlier = pltpu.roll(total, rows - shift, 0), pltpu.roll(total, shift, 0)
    total_ref[...] = total
    sent[...] = jnp.where((row & shift) == 0, later, earlier).astype(sent.dtype)


def combine(kernel, kept, got, out_rows, limit, waits_for=()):
    shape = (out_rows, kept.shape[1])
    shapes = (jax.ShapeDtypeStruct(shape, jnp.float32), jax.ShapeDtypeStruct(shape, jnp.bfloat16))
    return small_call(kernel, (kept, got), shapes, waits_for, limit)


def norm_kernel(kept, got, gain, residual, moe_in):
    rows_dev, width = residual.shape
    total = kept[...] + got[...].astype(jnp.float32)
    body = total[:, :width]
    square = jnp.mean(body * body, axis=1, keepdims=True)
    residual[...] = body[:rows_dev]
    moe_in[:, :width] = (body * lax.rsqrt(square + norm_eps) * gain[...]).astype(moe_in.dtype)
    moe_in[:, width:] = total[:, width:].astype(moe_in.dtype)


def norm(kept, got, gain, rows_dev, limit, waits_for):
    shapes = (
        jax.ShapeDtypeStruct((rows_dev, gain.shape[1]), jnp.float32),
        jax.ShapeDtypeStruct(kept.shape, jnp.bfloat16),
    )
    return small_call(norm_kernel, (kept, got, gain), shapes, waits_for, limit)


def stack_kernel(first, second, out):
    rows = first.shape[0]
    out[:rows] = first[...]
    out[rows:] = second[...]


def stack(first, second, limit, waits_for):
    shape = jax.ShapeDtypeStruct((2 * first.shape[0], first.shape[1]), first.dtype)
    return small_call(stack_kernel, (first, second), (shape,), waits_for, limit)[0]


def strips(source, target, sems):
    count = sems.shape[0]
    run = source.shape[1] // count
    return [
        pltpu.make_async_copy(
            source.at[:, pl.ds(i * run, run)], target.at[:, pl.ds(i * run, run)], sems.at[i]
        )
        for i in range(count)
    ]


def expert_kernel(
    me, first, second, gate_top, gate_bottom, up_top, up_bottom, down, kept, sent, moe_in, units, down_in, sems
):
    cut, inner = gate_top.shape
    width = 2 * cut
    half = kept.shape[0]
    downs = strips(down, down_in, sems)
    for copy in downs:
        copy.start()
    moe_in[:half] = first[...]
    moe_in[half:] = second[...]
    tail = moe_in[:, width:].astype(jnp.float32)
    column = lax.broadcasted_iota(jnp.int32, tail.shape, 1)
    expert = lax.rem(me[0], EXPERTS)
    mine = (column == expert) | (column == expert + EXPERTS)
    weight = jnp.sum(jnp.where(mine, tail, 0.0), axis=1, keepdims=True)

    def product(top, bottom, columns):
        return jnp.dot(
            moe_in[:, :cut], top[:, columns], preferred_element_type=jnp.float32
        ) + jnp.dot(moe_in[:, cut:width], bottom[:, columns], preferred_element_type=jnp.float32)

    strip = inner // 2

    @pl.loop(0, 2)
    def _(i):
        columns = pl.ds(pl.multiple_of(i * strip, strip), strip)
        gate_act = product(gate_top, gate_bottom, columns)
        up_act = product(up_top, up_bottom, columns)
        units[:, columns] = (jax.nn.silu(gate_act) * up_act).astype(units.dtype)
    for copy in downs:
        copy.wait()

    @pl.loop(0, 2)
    def _(i):
        columns = pl.ds(pl.multiple_of(i * cut, cut), cut)
        terms = weight * jnp.dot(
            units[...], down_in[:, columns], preferred_element_type=jnp.float32
        )
        kept[:, columns] = terms[:half]
        sent[:, columns] = terms[half:].astype(sent.dtype)


def run_expert(me, first, second, gate, up, down, limit):
    rows = 2 * first.shape[0]
    inner, width = down.shape
    shape = (rows // 2, width)
    return pl.pallas_call(
        expert_kernel,
        out_shape=(
            jax.ShapeDtypeStruct(shape, jnp.float32),
            jax.ShapeDtypeStruct(shape, jnp.bfloat16),
        ),
        in_specs=[IN_SMEM] + [IN_VMEM] * 6 + [IN_HBM],
        out_specs=(IN_VMEM, IN_VMEM),
        scratch_shapes=[
            pltpu.VMEM((rows, first.shape[1]), jnp.bfloat16),
            pltpu.VMEM((rows, inner), jnp.bfloat16),
            pltpu.VMEM(down.shape, down.dtype),
            pltpu.SemaphoreType.DMA((4,)),
        ],
        compiler_params=pltpu.CompilerParams(vmem_limit_bytes=limit + 2 * down.size),
    )(me, first, second, *[in_vmem(w) for w in gate + up], in_hbm(down))


def on_device(
    hidden,
    queries,
    latent_cache,
    cache_lengths,
    value_up,
    out_proj,
    norm_gain,
    expert_ids,
    gate_weights,
    gate_proj,
    up_proj,
    down_proj,
):
    rows_dev, width = hidden.shape
    ep_size = lax.axis_size("ep")
    me = lax.axis_index("ep")
    bits = ep_size.bit_length() - 1
    split_ways = ep_size // EXPERTS
    scatter_bits = min(2, bits)
    heads_dev, latent, _ = value_up.shape
    rows_in = ep_size * rows_dev

    experts_iota = lax.broadcasted_iota(jnp.int32, (1, 1, EXPERTS), 2)
    named = expert_ids[:, :, None] == experts_iota
    weight = jnp.sum(jnp.where(named, gate_weights[:, :, None], 0.0), axis=1)
    weight_top = weight.astype(jnp.bfloat16).astype(jnp.float32)
    weight_rest = (weight - weight_top).astype(jnp.bfloat16).astype(jnp.float32)
    tail = jnp.concatenate((weight_top, weight_rest), axis=1)
    tail = jnp.pad(tail, ((0, 0), (0, LANES - tail.shape[1])))

    order = relative_order(bits)
    limit = grant(rows_in, width)
    gate, up, down = gate_proj[0], up_proj[0], down_proj[0]
    if heads_dev % 8 == 0:
        kept, sent, value_up = attend(queries, latent_cache, cache_lengths, value_up, order, me)
        run = ep_size >> 2
        got = exchange(sent, 0)
        kept, sent = deal((kept, got), 2, run, limit)
        got = exchange(sent, 1)
        top, token = load(out_proj, sent, limit, 0)
        parts = deal((kept, got), run, 1, limit, (token,))
        bottom, _ = load(out_proj, parts[0], limit, 1)
        masks = order[:run]
        by_head = [parts[0]] + [trade(part, mask) for part, mask in zip(parts[1:], masks[1:])]
        held = [mask | x << 1 | core for mask in masks for x in range(2) for core in range(2)]
        row_of = jnp.array([held.index(s) * rows_dev + r for s in order for r in range(rows_dev)])
    else:
        out, _, value_up = attend(queries, latent_cache, cache_lengths, value_up, (), me)
        top, _ = load(out_proj, value_up, limit, 0)
        bottom, _ = load(out_proj, value_up, limit, 1)
        out = out.reshape(rows_dev, ep_size, heads_dev, latent).transpose(1, 0, 2, 3)
        by_head = [lax.all_to_all(out, "ep", split_axis=0, concat_axis=0, tiled=True)]
        by_head = [by_head[0].reshape(rows_in * heads_dev, latent)]
        row_of = (jnp.array(order) ^ me)[:, None] * rows_dev + jnp.arange(rows_dev)[None, :]
        row_of = row_of.reshape(-1)
    row_of = row_of.astype(jnp.int32)
    kept, sent = project(
        by_head, row_of[:, None], value_up, top, bottom, hidden, tail, limit
    )
    halves, later = [], [(w, part) for w in (gate, up) for part in range(2)]
    if split_ways > 1:
        later = []

    def beside(value):
        if not later:
            return ()
        source, part = later.pop(0)
        half, token = load(source, value, limit, part)
        halves.append(half)
        return (token,)


    rows = rows_in // 2
    for bit in range(scatter_bits - 1):
        rows //= 2
        kept, sent = combine(halve_kernel, kept, exchange(sent, bit), rows, limit)
    got = exchange(sent, scatter_bits - 1)
    for bit in range(scatter_bits, bits):
        swap = functools.partial(swap_kernel, rows_dev << (bits - 1 - bit))
        kept, sent = combine(swap, kept, got, rows, limit, beside(sent))
        got = exchange(sent, bit)
    residual, moe_in = norm(kept, got, norm_gain[None, :], rows_dev, limit, beside(sent))
    for bit in reversed(range(1, scatter_bits)):
        got = exchange(moe_in, bit)
        moe_in = stack(moe_in, got, limit, beside(moe_in))
    other = exchange(moe_in, 0)

    if split_ways == 1:
        while later:
            beside(moe_in)
        kept, sent = run_expert(me[None], moe_in, other, halves[:2], halves[2:], down, limit)
    else:
        moe_in = jnp.concatenate((moe_in, other), axis=0)
        expert = me % EXPERTS
        tail_in = moe_in[:, width:].astype(jnp.float32)
        column = lax.broadcasted_iota(jnp.int32, tail_in.shape, 1)
        mine = (column == expert) | (column == expert + EXPERTS)
        row_weight = jnp.sum(jnp.where(mine, tail_in, 0.0), axis=1, keepdims=True)
        slice_width = width // split_ways
        start = (me // EXPERTS) * slice_width
        part_in = lax.dynamic_slice_in_dim(moe_in, start, slice_width, axis=1)
        gate_act = jnp.dot(part_in, gate, preferred_element_type=jnp.float32)
        up_act = jnp.dot(part_in, up, preferred_element_type=jnp.float32)
        to_one = (row_of[:, None] == jnp.arange(rows_in)[None, :]).astype(jnp.float32)
        stacked = jnp.stack((gate_act, up_act)).astype(jnp.bfloat16).astype(jnp.float32)
        stacked = jnp.einsum("sr,asf->arf", to_one, stacked)
        for bit in range(EXPERTS.bit_length() - 1, bits):
            stacked = stacked + exchange(stacked.astype(jnp.bfloat16), bit).astype(jnp.float32)
        stacked = jnp.einsum("sr,arf->asf", to_one, stacked, precision=lax.Precision.HIGHEST)
        units = (jax.nn.silu(stacked[0]) * stacked[1]).astype(jnp.bfloat16)
        weighted = jnp.dot(units, down, preferred_element_type=jnp.float32) * row_weight
        spread = jnp.zeros((rows_in, width), jnp.float32)
        spread = lax.dynamic_update_slice_in_dim(spread, weighted, start, axis=1)
        kept, sent = spread[: rows_in // 2], spread[rows_in // 2 :].astype(jnp.bfloat16)
    rows = rows_in // 2
    for bit in range(bits - 1):
        rows //= 2
        kept, sent = combine(halve_kernel, kept, exchange(sent, bit), rows, limit)
    routed = kept + exchange(sent, bits - 1).astype(jnp.float32)
    return (residual + routed).astype(jnp.bfloat16)


def solution(mesh):
    return jax.shard_map(
        on_device,
        mesh=mesh,
        in_specs=(
            P(("groups", "ep"), None),
            P(("groups", "ep"), None, None),
            P(("groups", "ep"), None, None),
            P(("groups", "ep")),
            P("ep", None, None),
            P("ep", None),
            P(),
            P(("groups", "ep"), None),
            P(("groups", "ep"), None),
            P("ep", None, None),
            P("ep", None, None),
            P("ep", None, None),
        ),
        out_specs=P(("groups", "ep"), None),
        check_vma=False,
    )
```

```python
import functools

import jax
import jax.numpy as jnp
from jax import lax
from jax.experimental import pallas as pl
from jax.experimental.pallas import tpu as pltpu
from jax.sharding import PartitionSpec as P

EXPERTS = 16


score_scale = 0.07216878364870323
norm_eps = 1e-06


def exchange(value, bit):
    return trade(value, 1 << bit)


def trade(value, mask):
    return lax.ppermute(value, "ep", [(i, i ^ mask) for i in range(lax.axis_size("ep"))])


def relative_order(bits):
    return [sum(((p >> (bits - 1 - b)) & 1) << b for b in range(bits)) for p in range(1 << bits)]


LANES = 128
MIB = 1 << 20
IN_VMEM = pl.BlockSpec(memory_space=pltpu.VMEM)
IN_HBM = pl.BlockSpec(memory_space=pltpu.HBM)
VMEM_ARRAY = pltpu.VMEM


def in_vmem(value):
    return pltpu.with_memory_space_constraint(value, pltpu.VMEM)


def in_hbm(value):
    return pltpu.with_memory_space_constraint(value, pltpu.HBM)


def pieces(source, target, sems, first):
    count = sems.shape[0] - first
    run = source.shape[0] // count
    return [
        pltpu.make_async_copy(
            source.at[pl.ds(i * run, run)], target.at[pl.ds(i * run, run)], sems.at[first + i]
        )
        for i in range(count)
    ]


def load_kernel(first, source, after, target, done, sems):
    done[...] = jnp.zeros_like(done)
    copies = pieces(source.at[pl.ds(first, target.shape[0])], target, sems, 0)
    for copy in copies:
        copy.start()
    for copy in copies:
        copy.wait()


def load(source, after, limit, part, parts=2):
    rows = source.shape[0] // parts
    return pl.pallas_call(
        functools.partial(load_kernel, part * rows),
        out_shape=(
            VMEM_ARRAY((rows, source.shape[1]), source.dtype),
            VMEM_ARRAY((8, LANES), jnp.float32),
        ),
        in_specs=[IN_HBM, IN_VMEM],
        out_specs=(IN_VMEM, IN_VMEM),
        scratch_shapes=[pltpu.SemaphoreType.DMA((4,))],
        compiler_params=pltpu.CompilerParams(vmem_limit_bytes=limit),
        cost_estimate=pl.CostEstimate(
            flops=0,
            bytes_accessed=2 * rows * source.shape[1] * source.dtype.itemsize,
            transcendentals=0,
        ),
    )(in_hbm(source), in_vmem(after))


def grant(rows, columns):
    return 4 * MIB + 16 * rows * columns


def only(kernel, ins, outs, *refs):
    kernel(*refs[:ins], *refs[len(refs) - outs :])


def small_call(kernel, operands, shapes, waits_for, limit):
    ins, outs = len(operands), len(shapes)
    return pl.pallas_call(
        functools.partial(only, kernel, ins, outs),
        out_shape=tuple(shapes),
        in_specs=[IN_VMEM] * (ins + len(waits_for)),
        out_specs=(IN_VMEM,) * outs,
        compiler_params=pltpu.CompilerParams(vmem_limit_bytes=limit),
    )(*operands, *waits_for)


def attend_kernel(
    order, lengths_hbm, queries_hbm, cache, value_up, kept, sent, value_in, lengths, queries, held, wide, sems
):
    rows_dev, _, heads = queries.shape
    context = cache.shape[2]
    latent = wide.shape[-1]
    caches = [pltpu.make_async_copy(cache.at[r], held.at[r], sems.at[r]) for r in range(rows_dev)]
    first = [
        pltpu.make_async_copy(lengths_hbm, lengths, sems.at[rows_dev]),
        pltpu.make_async_copy(queries_hbm, queries, sems.at[rows_dev + 1]),
    ]
    weights = pltpu.make_async_copy(value_up, value_in, sems.at[rows_dev + 2])
    for copy in first + caches + [weights]:
        copy.start()
    for copy in first:
        copy.wait()
    for r in range(rows_dev):
        caches[r].wait()
        scores = score_scale * lax.dot_general(
            queries[r], held[r], (((0,), (0,)), ((), ())), preferred_element_type=jnp.float32
        )
        positions = lax.broadcasted_iota(jnp.int32, (heads, context), 1)
        scores = jnp.where(positions < lengths[r], scores, -jnp.inf)
        exp_scores = jnp.exp(scores - jnp.max(scores, axis=1, keepdims=True))
        inverse = 1.0 / jnp.sum(exp_scores, axis=1, keepdims=True)
        got = inverse * lax.dot_general(
            exp_scores.astype(jnp.bfloat16),
            held[r, :latent],
            (((1,), (1,)), ((), ())),
            preferred_element_type=jnp.float32,
        )
        if order:
            per = wide.shape[1] // rows_dev
            wide[:, r * per : (r + 1) * per] = got.reshape(-1, per, latent)
        else:
            kept[r] = got.astype(kept.dtype)
    half = len(order) // 2
    me = lax.axis_index("ep")
    for p, s in enumerate(order):
        target = (kept, sent)[p // half]
        target[p % half] = wide[me ^ s].astype(target.dtype)
    weights.wait()


def attend(queries, latent_cache, cache_lengths, value_up, order):
    rows_dev, heads, key_width = queries.shape
    context = latent_cache.shape[1]
    heads_dev, latent, _ = value_up.shape
    shape = (len(order) // 2, rows_dev * heads_dev, latent) if order else (rows_dev, heads, latent)
    wide = (max(2 * shape[0], 1), shape[1], latent) if order else (1, 8, latent)
    spare = shape if order else (1, 16, latent)
    return pl.pallas_call(
        functools.partial(attend_kernel, order),
        out_shape=(
            VMEM_ARRAY(shape, jnp.bfloat16),
            VMEM_ARRAY(spare, jnp.bfloat16),
            VMEM_ARRAY(value_up.shape, value_up.dtype),
        ),
        in_specs=[IN_HBM] * 4,
        out_specs=(IN_VMEM,) * 3,
        scratch_shapes=[
            pltpu.SMEM((rows_dev,), jnp.int32),
            pltpu.VMEM((rows_dev, key_width, heads), jnp.bfloat16),
            pltpu.VMEM((rows_dev, key_width, context), jnp.bfloat16),
            pltpu.VMEM(wide, jnp.float32),
            pltpu.SemaphoreType.DMA((rows_dev + 3,)),
        ],
        compiler_params=pltpu.CompilerParams(vmem_limit_bytes=24 * MIB),
    )(
        in_hbm(cache_lengths),
        in_hbm(queries.transpose(0, 2, 1)),
        in_hbm(latent_cache.transpose(0, 2, 1)),
        in_hbm(value_up),
    )


def dealt(sources, ways, run):
    return [
        [
            (a, (g * ways + i) * run)
            for a, blocks in enumerate(sources)
            for g in range(blocks // (ways * run))
        ]
        for i in range(ways)
    ]


def deal_kernel(plan, run, count, *refs):
    sources, targets = refs[:count], refs[-len(plan) :]
    for target, runs in zip(targets, plan):
        for j, (a, first) in enumerate(runs):
            target[j * run : (j + 1) * run] = sources[a][first : first + run]


def deal(sources, ways, run, limit, waits_for=()):
    plan = dealt([a.shape[0] for a in sources], ways, run)
    shape = (len(plan[0]) * run, *sources[0].shape[1:])
    return pl.pallas_call(
        functools.partial(deal_kernel, plan, run, len(sources)),
        out_shape=tuple(jax.ShapeDtypeStruct(shape, sources[0].dtype) for _ in plan),
        in_specs=[IN_VMEM] * (len(sources) + len(waits_for)),
        out_specs=(IN_VMEM,) * ways,
        compiler_params=pltpu.CompilerParams(vmem_limit_bytes=limit),
    )(*sources, *waits_for)


def project_kernel(tile, count, *refs):
    row_of, value_up, top, bottom, hidden, tail, kept, sent = refs[count:]
    heads_dev = value_up.shape[0]
    half, wide = kept.shape
    rows_dev, width = hidden.shape
    maps = jnp.concatenate([value_up[h] for h in range(heads_dev)], axis=1)
    by_head = jnp.concatenate([a[...].reshape(-1, a.shape[-1]) for a in refs[:count]], axis=0)
    mixed = jnp.dot(by_head, maps, preferred_element_type=jnp.float32)
    row_head = lax.rem(lax.broadcasted_iota(jnp.int32, mixed.shape, 0), heads_dev)
    value_dim = value_up.shape[2]
    column_head = lax.broadcasted_iota(jnp.int32, mixed.shape, 1) // value_dim
    mixed = jnp.where(row_head == column_head, mixed, 0.0).astype(jnp.bfloat16)
    source = lax.broadcasted_iota(jnp.int32, (2 * half, mixed.shape[0]), 1) // heads_dev
    select = (row_of[...] == source).astype(jnp.bfloat16)
    head_rows = jnp.dot(select, mixed, preferred_element_type=jnp.float32)
    head_rows = head_rows.astype(jnp.bfloat16)
    cut = top.shape[0]

    @pl.loop(0, width // tile)
    def _(i):
        columns = pl.ds(pl.multiple_of(i * tile, tile), tile)
        terms = jnp.dot(head_rows[:, :cut], top[:, columns], preferred_element_type=jnp.float32)
        terms += jnp.dot(
            head_rows[:, cut:], bottom[:, columns], preferred_element_type=jnp.float32
        )
        kept[:, columns] = terms[:half]
        kept[0:rows_dev, columns] += hidden[:, columns].astype(jnp.float32)
        sent[:, columns] = terms[half:].astype(sent.dtype)

    kept[:, width:] = jnp.zeros((half, wide - width), kept.dtype)
    kept[0:rows_dev, width:] = tail[...]
    sent[:, width:] = jnp.zeros((half, wide - width), sent.dtype)


def project(by_head, row_of, value_up, top, bottom, hidden, tail, limit):
    rows_in = row_of.shape[0]
    width = hidden.shape[1]
    shape = (rows_in // 2, width + LANES)
    return pl.pallas_call(
        functools.partial(project_kernel, width // 2, len(by_head)),
        out_shape=(
            jax.ShapeDtypeStruct(shape, jnp.float32),
            jax.ShapeDtypeStruct(shape, jnp.bfloat16),
        ),
        in_specs=[IN_VMEM] * (len(by_head) + 6),
        out_specs=(IN_VMEM, IN_VMEM),
        compiler_params=pltpu.CompilerParams(vmem_limit_bytes=limit),
    )(
        *by_head,
        row_of,
        in_vmem(value_up),
        in_vmem(top),
        in_vmem(bottom),
        hidden,
        tail,
    )


def halve_kernel(kept, got, next_kept, sent):
    half = sent.shape[0]
    total = kept[...] + got[...].astype(jnp.float32)
    next_kept[...] = total[:half]
    sent[...] = total[half:].astype(sent.dtype)


def swap_kernel(shift, kept, got, total_ref, sent):
    total = kept[...] + got[...].astype(jnp.float32)
    rows = total.shape[0]
    row = lax.broadcasted_iota(jnp.int32, total.shape, 0)
    later, earlier = pltpu.roll(total, rows - shift, 0), pltpu.roll(total, shift, 0)
    total_ref[...] = total
    sent[...] = jnp.where((row & shift) == 0, later, earlier).astype(sent.dtype)


def combine(kernel, kept, got, out_rows, limit, waits_for=()):
    shape = (out_rows, kept.shape[1])
    shapes = (jax.ShapeDtypeStruct(shape, jnp.float32), jax.ShapeDtypeStruct(shape, jnp.bfloat16))
    return small_call(kernel, (kept, got), shapes, waits_for, limit)


def norm_kernel(kept, got, gain, residual, moe_in):
    rows_dev, width = residual.shape
    total = kept[...] + got[...].astype(jnp.float32)
    body = total[:, :width]
    square = jnp.mean(body * body, axis=1, keepdims=True)
    residual[...] = body[:rows_dev]
    moe_in[:, :width] = (body * lax.rsqrt(square + norm_eps) * gain[...]).astype(moe_in.dtype)
    moe_in[:, width:] = total[:, width:].astype(moe_in.dtype)


def norm(kept, got, gain, rows_dev, limit, waits_for):
    shapes = (
        jax.ShapeDtypeStruct((rows_dev, gain.shape[1]), jnp.float32),
        jax.ShapeDtypeStruct(kept.shape, jnp.bfloat16),
    )
    return small_call(norm_kernel, (kept, got, gain), shapes, waits_for, limit)


def stack_kernel(first, second, out):
    rows = first.shape[0]
    out[:rows] = first[...]
    out[rows:] = second[...]


def stack(first, second, limit, waits_for):
    shape = jax.ShapeDtypeStruct((2 * first.shape[0], first.shape[1]), first.dtype)
    return small_call(stack_kernel, (first, second), (shape,), waits_for, limit)[0]


def strips(source, target, sems):
    count = sems.shape[0]
    run = source.shape[1] // count
    return [
        pltpu.make_async_copy(
            source.at[:, pl.ds(i * run, run)], target.at[:, pl.ds(i * run, run)], sems.at[i]
        )
        for i in range(count)
    ]


def expert_kernel(
    first, second, gate_top, gate_bottom, up_top, up_bottom, down, kept, sent, moe_in, units, down_in, sems
):
    cut, inner = gate_top.shape
    width = 2 * cut
    half = kept.shape[0]
    downs = strips(down, down_in, sems)
    for copy in downs:
        copy.start()
    moe_in[:half] = first[...]
    moe_in[half:] = second[...]
    tail = moe_in[:, width:].astype(jnp.float32)
    column = lax.broadcasted_iota(jnp.int32, tail.shape, 1)
    expert = lax.rem(lax.axis_index("ep"), EXPERTS)
    mine = (column == expert) | (column == expert + EXPERTS)
    weight = jnp.sum(jnp.where(mine, tail, 0.0), axis=1, keepdims=True)

    def product(top, bottom, columns):
        return jnp.dot(
            moe_in[:, :cut], top[:, columns], preferred_element_type=jnp.float32
        ) + jnp.dot(moe_in[:, cut:width], bottom[:, columns], preferred_element_type=jnp.float32)

    strip = inner // 2

    @pl.loop(0, 2)
    def _(i):
        columns = pl.ds(pl.multiple_of(i * strip, strip), strip)
        gate_act = product(gate_top, gate_bottom, columns)
        up_act = product(up_top, up_bottom, columns)
        units[:, columns] = (jax.nn.silu(gate_act) * up_act).astype(units.dtype)
    for copy in downs:
        copy.wait()

    @pl.loop(0, 2)
    def _(i):
        columns = pl.ds(pl.multiple_of(i * cut, cut), cut)
        terms = weight * jnp.dot(
            units[...], down_in[:, columns], preferred_element_type=jnp.float32
        )
        kept[:, columns] = terms[:half]
        sent[:, columns] = terms[half:].astype(sent.dtype)


def run_expert(first, second, gate, up, down, limit):
    rows = 2 * first.shape[0]
    inner, width = down.shape
    shape = (rows // 2, width)
    return pl.pallas_call(
        expert_kernel,
        out_shape=(
            jax.ShapeDtypeStruct(shape, jnp.float32),
            jax.ShapeDtypeStruct(shape, jnp.bfloat16),
        ),
        in_specs=[IN_VMEM] * 6 + [IN_HBM],
        out_specs=(IN_VMEM, IN_VMEM),
        scratch_shapes=[
            pltpu.VMEM((rows, first.shape[1]), jnp.bfloat16),
            pltpu.VMEM((rows, inner), jnp.bfloat16),
            pltpu.VMEM(down.shape, down.dtype),
            pltpu.SemaphoreType.DMA((4,)),
        ],
        compiler_params=pltpu.CompilerParams(vmem_limit_bytes=limit + 2 * down.size),
    )(first, second, *[in_vmem(w) for w in gate + up], in_hbm(down))


def on_device(
    hidden,
    queries,
    latent_cache,
    cache_lengths,
    value_up,
    out_proj,
    norm_gain,
    expert_ids,
    gate_weights,
    gate_proj,
    up_proj,
    down_proj,
):
    rows_dev, width = hidden.shape
    ep_size = lax.axis_size("ep")
    me = lax.axis_index("ep")
    bits = ep_size.bit_length() - 1
    split_ways = ep_size // EXPERTS
    scatter_bits = min(2, bits)
    heads_dev, latent, _ = value_up.shape
    rows_in = ep_size * rows_dev

    experts_iota = lax.broadcasted_iota(jnp.int32, (1, 1, EXPERTS), 2)
    named = expert_ids[:, :, None] == experts_iota
    weight = jnp.sum(jnp.where(named, gate_weights[:, :, None], 0.0), axis=1)
    weight_top = weight.astype(jnp.bfloat16).astype(jnp.float32)
    weight_rest = (weight - weight_top).astype(jnp.bfloat16).astype(jnp.float32)
    tail = jnp.concatenate((weight_top, weight_rest), axis=1)
    tail = jnp.pad(tail, ((0, 0), (0, LANES - tail.shape[1])))

    order = relative_order(bits)
    limit = grant(rows_in, width)
    gate, up, down = gate_proj[0], up_proj[0], down_proj[0]
    if heads_dev % 8 == 0:
        kept, sent, value_up = attend(queries, latent_cache, cache_lengths, value_up, order)
        run = ep_size >> 2
        got = exchange(sent, 0)
        kept, sent = deal((kept, got), 2, run, limit)
        got = exchange(sent, 1)
        top, token = load(out_proj, sent, limit, 0)
        parts = deal((kept, got), run, 1, limit, (token,))
        bottom, _ = load(out_proj, parts[0], limit, 1)
        masks = order[:run]
        by_head = [parts[0]] + [trade(part, mask) for part, mask in zip(parts[1:], masks[1:])]
        held = [mask | x << 1 | core for mask in masks for x in range(2) for core in range(2)]
        row_of = jnp.array([held.index(s) * rows_dev + r for s in order for r in range(rows_dev)])
    else:
        out, _, value_up = attend(queries, latent_cache, cache_lengths, value_up, ())
        top, _ = load(out_proj, value_up, limit, 0)
        bottom, _ = load(out_proj, value_up, limit, 1)
        out = out.reshape(rows_dev, ep_size, heads_dev, latent).transpose(1, 0, 2, 3)
        by_head = [lax.all_to_all(out, "ep", split_axis=0, concat_axis=0, tiled=True)]
        by_head = [by_head[0].reshape(rows_in * heads_dev, latent)]
        row_of = (jnp.array(order) ^ me)[:, None] * rows_dev + jnp.arange(rows_dev)[None, :]
        row_of = row_of.reshape(-1)
    row_of = row_of.astype(jnp.int32)
    kept, sent = project(
        by_head, row_of[:, None], value_up, top, bottom, hidden, tail, limit
    )
    halves, later = [], [(w, part) for w in (gate, up) for part in range(2)]
    if split_ways > 1:
        later = []

    def beside(value):
        if not later:
            return ()
        source, part = later.pop(0)
        half, token = load(source, value, limit, part)
        halves.append(half)
        return (token,)


    rows = rows_in // 2
    for bit in range(scatter_bits - 1):
        rows //= 2
        kept, sent = combine(halve_kernel, kept, exchange(sent, bit), rows, limit)
    got = exchange(sent, scatter_bits - 1)
    for bit in range(scatter_bits, bits):
        swap = functools.partial(swap_kernel, rows_dev << (bits - 1 - bit))
        kept, sent = combine(swap, kept, got, rows, limit, beside(sent))
        got = exchange(sent, bit)
    residual, moe_in = norm(kept, got, norm_gain[None, :], rows_dev, limit, beside(sent))
    for bit in reversed(range(1, scatter_bits)):
        got = exchange(moe_in, bit)
        moe_in = stack(moe_in, got, limit, beside(moe_in))
    other = exchange(moe_in, 0)

    if split_ways == 1:
        while later:
            beside(moe_in)
        kept, sent = run_expert(moe_in, other, halves[:2], halves[2:], down, limit)
    else:
        moe_in = jnp.concatenate((moe_in, other), axis=0)
        expert = me % EXPERTS
        tail_in = moe_in[:, width:].astype(jnp.float32)
        column = lax.broadcasted_iota(jnp.int32, tail_in.shape, 1)
        mine = (column == expert) | (column == expert + EXPERTS)
        row_weight = jnp.sum(jnp.where(mine, tail_in, 0.0), axis=1, keepdims=True)
        slice_width = width // split_ways
        start = (me // EXPERTS) * slice_width
        part_in = lax.dynamic_slice_in_dim(moe_in, start, slice_width, axis=1)
        gate_act = jnp.dot(part_in, gate, preferred_element_type=jnp.float32)
        up_act = jnp.dot(part_in, up, preferred_element_type=jnp.float32)
        to_one = (row_of[:, None] == jnp.arange(rows_in)[None, :]).astype(jnp.float32)
        stacked = jnp.stack((gate_act, up_act)).astype(jnp.bfloat16).astype(jnp.float32)
        stacked = jnp.einsum("sr,asf->arf", to_one, stacked)
        for bit in range(EXPERTS.bit_length() - 1, bits):
            stacked = stacked + exchange(stacked.astype(jnp.bfloat16), bit).astype(jnp.float32)
        stacked = jnp.einsum("sr,arf->asf", to_one, stacked, precision=lax.Precision.HIGHEST)
        units = (jax.nn.silu(stacked[0]) * stacked[1]).astype(jnp.bfloat16)
        weighted = jnp.dot(units, down, preferred_element_type=jnp.float32) * row_weight
        spread = jnp.zeros((rows_in, width), jnp.float32)
        spread = lax.dynamic_update_slice_in_dim(spread, weighted, start, axis=1)
        kept, sent = spread[: rows_in // 2], spread[rows_in // 2 :].astype(jnp.bfloat16)
    rows = rows_in // 2
    for bit in range(bits - 1):
        rows //= 2
        kept, sent = combine(halve_kernel, kept, exchange(sent, bit), rows, limit)
    routed = kept + exchange(sent, bits - 1).astype(jnp.float32)
    return (residual + routed).astype(jnp.bfloat16)


def solution(mesh):
    return jax.shard_map(
        on_device,
        mesh=mesh,
        in_specs=(
            P(("groups", "ep"), None),
            P(("groups", "ep"), None, None),
            P(("groups", "ep"), None, None),
            P(("groups", "ep")),
            P("ep", None, None),
            P("ep", None),
            P(),
            P(("groups", "ep"), None),
            P(("groups", "ep"), None),
            P("ep", None, None),
            P("ep", None, None),
            P("ep", None, None),
        ),
        out_specs=P(("groups", "ep"), None),
        check_vma=False,
    )
```
